256 devices in a mesh: dp: 4 (over x), fsdp: 64 (over y, z, core).
Axes of the slice: x: 4, y: 4, z: 8, core: 2. Of those that a mesh axis runs over, the one named last changes fastest.
Arguments:
- hidden: bfloat16 [512, 4096], P('dp', 'fsdp'), may hold values from -6 to 6
- grad_query: bfloat16 [512, 4096], P('dp', 'fsdp'), may hold values from -6 to 6
- attn_out: bfloat16 [512, 4096], P('dp', 'fsdp'), may hold values from -6 to 6
- grad_output: bfloat16 [512, 4096], P('dp', 'fsdp'), may hold values from -6 to 6
- flat_params: float32 [33558528], P('fsdp')
- moment_one: float32 [33558528], P('fsdp'), may hold values from -192 to 192
- moment_two: float32 [33558528], P('fsdp'), may hold values from 20 to 400
- step_count: int32 [1], replicated, may hold values from 1 to 19
Outputs:
- grad_hidden: bfloat16 [512, 4096], P('dp', 'fsdp')
- grad_attn: bfloat16 [512, 4096], P('dp', 'fsdp')
- new_params: float32 [33558528], P('fsdp')
- new_moment_one: float32 [33558528], P('fsdp')
- new_moment_two: float32 [33558528], P('fsdp')
The draws below stay inside these ranges and needn't reach their ends.
All inputs are finite; a program needn't handle non-finite values.
Results may differ from the reference program's by a relative error of at most 0.0012.
The reference program's roundings to bfloat16 on the way count: a program that leaves them out, or rounds other values in their place, can miss the bound.
Values may be sent and summed in bfloat16 or wider, within the bound.
A program may use at most 128 MiB of HBM per device.

```python
import math
import jax
import jax.numpy as jnp
from jax import lax

NHEAD = 32
HD = 128
D = 4096
TOKENS = 512
FLAT = 33558528


def draw_flat_params(key, part):
    key = jax.random.fold_in(key, 11)
    gain_key, value_key = jax.random.split(key)
    flat_len = D * (2 * D + 1)
    exponent = jax.random.uniform(gain_key, (NHEAD,), jnp.float32, -1.0, 1.0)
    head_gain = jnp.exp(exponent * math.log(2.0))
    values = jnp.clip(jax.random.normal(value_key, (flat_len,), jnp.float32), -6.0, 6.0)
    positions = jnp.arange(flat_len, dtype=jnp.int32)
    row_ids = positions // D
    col_ids = positions - row_ids * D
    head_ids = jnp.where(row_ids < D, row_ids // HD, col_ids // HD)
    rising = 0.5 + positions.astype(jnp.float32) / flat_len
    factor = head_gain[head_ids] * rising / math.sqrt(D)
    return values * factor


def level_of(rng, dims, cuts, smallest, largest):
    def one(position, parts):
        heights = jax.random.uniform(jax.random.fold_in(jax.random.fold_in(rng, 6), position), (parts,), jnp.float32, smallest / len(cuts), largest / len(cuts))
        return jnp.repeat(jnp.exp(heights), dims[position] // parts).reshape((-1,) + (1,) * (len(dims) - position - 1))

    loudness = one(*cuts[0])
    for cut in cuts[1:]:
        loudness = loudness * one(*cut)
    return loudness


def noise(key, shape, deviation, bound, pieces=(), kind=jnp.bfloat16):
    values = deviation * jax.random.normal(key, shape, jnp.float32)
    if pieces:
        values = values * level_of(key, shape, pieces, -0.22, 0.18)
    return jnp.clip(values, -bound, bound).astype(kind)


def setup_inputs(seed: int = 0) -> dict:
    key_of = jax.random.split(jax.random.key(seed), 9)
    hidden = noise(key_of[0], (TOKENS, D), 1.0, 6.0, ((0, 4), (1, 64)))
    grad_query = noise(key_of[1], (TOKENS, D), 1.0, 6.0, ((0, 4), (1, 64)))
    attn_out = noise(key_of[2], (TOKENS, D), 1.0, 6.0, ((0, 4), (1, 64)))
    grad_output = noise(key_of[3], (TOKENS, D), 1.0, 6.0, ((0, 4), (1, 64)))
    flat_params = draw_flat_params(jax.random.fold_in(key_of[8], 71), 0)
    moment_one = noise(key_of[5], (FLAT,), 30.0, 192.0, ((0, 64),), jnp.float32)
    moment_two = jnp.clip(jnp.exp(math.log(400.0) - 2.9957323 * jax.random.uniform(key_of[6], (FLAT,), jnp.float32) ** level_of(key_of[6], (FLAT,), ((0, 64),), -0.2, 0.2)), 20.0, 400.0)
    step_count = jax.random.randint(key_of[7], (1,), 1, 20).astype(jnp.int32)
    return dict(hidden=hidden, grad_query=grad_query, attn_out=attn_out, grad_output=grad_output, flat_params=flat_params, moment_one=moment_one, moment_two=moment_two, step_count=step_count)


beta_one = 0.9
beta_two = 0.95
adam_eps = 1e-08
learn_rate = 0.02
decay_rate = 0.1
lasso_weight = 2.0
norm_eps = 1e-06

def reference(hidden, grad_query, attn_out, grad_output, flat_params, moment_one, moment_two, step_count):
    square = D * D
    q_weight = flat_params[:square].reshape(D, D)
    o_weight = flat_params[square + D:].reshape(D, D)
    grad_qweight = jnp.dot(grad_query.T, hidden, preferred_element_type=jnp.float32)
    grad_qbias = lax.optimization_barrier(jnp.sum(grad_query.astype(jnp.float32), axis=0))
    grad_oweight = jnp.dot(grad_output.T, attn_out, preferred_element_type=jnp.float32)
    gradient = jnp.concatenate([grad_qweight.reshape(-1), grad_qbias, grad_oweight.reshape(-1)])
    grad_hidden = jnp.dot(grad_query, q_weight.astype(jnp.bfloat16), preferred_element_type=jnp.float32).astype(jnp.bfloat16)
    grad_attn = jnp.dot(grad_output, o_weight.astype(jnp.bfloat16), preferred_element_type=jnp.float32).astype(jnp.bfloat16)
    step_num = step_count[0].astype(jnp.float32)
    new_one = beta_one * moment_one + (1.0 - beta_one) * gradient
    new_two = beta_two * moment_two + (1.0 - beta_two) * gradient * gradient
    first_fix = 1.0 - jnp.power(jnp.float32(beta_one), step_num)
    second_fix = 1.0 - jnp.power(jnp.float32(beta_two), step_num)
    direction = new_one / first_fix / (jnp.sqrt(new_two / second_fix) + adam_eps)
    updated = flat_params - learn_rate * (direction + decay_rate * flat_params)
    q_part = updated[:square].reshape(NHEAD, HD * D)
    b_part = updated[square:square + D].reshape(NHEAD, HD)
    o_part = updated[square + D:].reshape(D, NHEAD, HD)
    sumsq = lax.optimization_barrier(jnp.sum(q_part * q_part, axis=1)) + lax.optimization_barrier(jnp.sum(b_part * b_part, axis=1)) + lax.optimization_barrier(jnp.sum(o_part * o_part, axis=(0, 2)))
    head_norm = jnp.sqrt(sumsq + norm_eps)
    threshold = learn_rate * lasso_weight * math.sqrt(2 * HD * D + HD)
    shrink = jnp.maximum(1.0 - threshold / head_norm, 0.0)
    new_params = jnp.concatenate([(q_part * shrink[:, None]).reshape(-1), (b_part * shrink[:, None]).reshape(-1), (o_part * shrink[None, :, None]).reshape(-1)])
    return (grad_hidden, grad_attn, new_params, new_one, new_two)
```

```python
import functools
import math

import jax
import jax.numpy as jnp
from jax import lax
from jax.experimental import pallas as pl
from jax.experimental.pallas import tpu as pltpu
from jax.sharding import PartitionSpec as P

HD = 128
NX = 4
NY = 4
CORES = 2
TOK = 128
BLK = 128

beta_one = 0.9
beta_two = 0.95
adam_eps = 1e-08
learn_rate = 0.02
decay_rate = 0.1
lasso_weight = 2.0
norm_eps = 1e-06

MESH = pl.DeviceIdType.MESH
F32 = jnp.float32
BF16 = jnp.bfloat16
NT = (((1,), (1,)), ((), ()))


def kernel(
    nz, hb, gb, ab, ob, tails, fixes, p_hbm, m1_hbm, m2_hbm,
    gh_out, ga_out, np_out, n1_out, n2_out,
    p1, m1, m2, p2, o1, o2, g2, gw,
    pack, rpack, xblk, lsend, lb, rg, lt, ll, lown,
    rbuf, pb, xs, xr, ring, yb, bias_own, bias_grp, bias_got,
    ext_ref, acc_ref, last_ref, s_own, s_grp, s_mid, s_col,
    in_sem, out_sem, s_sw, r_sw, s_ry, r_ry, s_lf, r_lf, s_lx, r_lx,
    s_bg, r_bg, s_by, r_by, s_rz, r_rz, s_r1, r_r1, s_r2, r_r2, s_rp, r_rp,
    s_sp, r_sp, s_sr, r_sr, s_sy, r_sy, s_sg, r_sg, s_ss, r_ss,
):
    nf = NY * nz * CORES
    nb = NY * nz
    dim = nb * BLK
    half_y = NY // 2
    longs, shorts = nz // 2, nz - 1 - nz // 2
    x = lax.axis_index("dp")
    f = lax.axis_index("fsdp")
    c = f % CORES
    z = (f // CORES) % nz
    y = f // (CORES * nz)
    h = y // half_y
    m = f // 2
    par = f % 2
    k = f // CORES
    sig = 1 - 2 * c

    def fid(yy, zz, cc):
        return (yy * nz + zz) * CORES + cc

    def zw(v):
        return (v + 2 * nz) % nz

    partner = fid(y, z, 1 - c)
    z_long = fid(y, zw(z + sig), c)
    z_short = fid(y, zw(z - sig), c)
    x_up = (x + 1) % NX
    x_down = (x + NX - 1) % NX
    x_far = (x + 2) % NX

    pending = []

    def send(src, dst, ss, rs, xx, ff):
        copy = pltpu.make_async_remote_copy(
            src_ref=src, dst_ref=dst, send_sem=ss, recv_sem=rs,
            device_id=(xx, ff), device_id_type=MESH,
        )
        copy.start()
        return copy

    def send_later(*args):
        pending.append(send(*args))

    def arrive(dst, rs):
        pltpu.make_async_remote_copy(
            src_ref=dst, dst_ref=dst, send_sem=s_sw, recv_sem=rs,
            device_id=(x, partner), device_id_type=MESH,
        ).wait_recv()

    cells = nb * BLK * BLK
    loads = [
        pltpu.make_async_copy(src.at[pl.ds(0, cells)], dst, in_sem.at[i])
        for i, (src, dst) in enumerate(((p_hbm, p1), (m1_hbm, m1), (m2_hbm, m2)))
    ]
    for load in loads:
        load.start()

    barrier = pltpu.get_barrier_semaphore()

    def greet(xx, ff):
        pl.semaphore_signal(barrier, inc=1, device_id=(xx, ff), device_id_type=MESH)

    group = [(dz, dc) for dz in range(nz) for dc in range(CORES) if (dz, dc) != (0, 0)]
    for dz, dc in group:
        greet(x, fid(y, zw(z + dz), (c + dc) % CORES))
    for dy in range(1, NY):
        for dc in range(CORES):
            greet(x, fid((y + dy) % NY, z, (c + dc) % CORES))
    for dx in range(1, NX):
        greet((x + dx) % NX, f)
    fl = f % (nf // 2)
    left_src = 2 * fl + h
    row_src = 2 * (fl + 1 - 2 * h) + h
    row_chip = fl + 1 - 2 * h
    has_row = (row_chip >= 0) & (row_chip < nf // 2)
    left_dst = c * (nf // 2) + k
    row_dst_low = k - 1 + 2 * c
    gives_row = (row_dst_low >= 0) & (row_dst_low < nf // 2)
    row_dst = c * (nf // 2) + row_dst_low

    @pl.when(left_src != f)
    def _():
        greet(x, left_src)

    @pl.when(has_row)
    def _():
        greet(x, row_src)

    own_pack = jnp.where(
        c == 0,
        jnp.concatenate([hb[...], gb[...]], axis=1).astype(F32),
        jnp.concatenate([ab[...], ob[...]], axis=1).astype(F32),
    )
    pack[...] = jnp.where(
        c == 0,
        jnp.concatenate([ab[...], ob[...]], axis=1).astype(F32),
        jnp.concatenate([hb[...], gb[...]], axis=1).astype(F32),
    ).astype(BF16)

    greeted = len(group) + (NY - 1) * CORES + NX - 1
    greeted = greeted + (left_dst != f).astype(jnp.int32) + gives_row.astype(jnp.int32)
    pl.semaphore_wait(barrier, greeted)

    send_later(pack, rpack, s_sw, r_sw, x, partner)
    lane = lax.broadcasted_iota(jnp.int32, (BLK, BLK), 1)
    row = lax.broadcasted_iota(jnp.int32, (BLK, BLK), 0)
    low = lane < 64
    arrive(rpack, r_sw)
    got = rpack[...].astype(F32)
    even = jnp.where(c == 0, own_pack, got)
    odd = jnp.where(c == 0, got, own_pack)
    right = jnp.where(low, even, pltpu.roll(odd, 64, 1))
    left = jnp.where(low, pltpu.roll(even, 64, 1), odd)
    xblk[...] = right.astype(BF16)

    for i in range(half_y):
        for cc in range(CORES):
            yd = half_y * c + i

            @pl.when((yd != y) | (cc != c))
            def _(i=i, cc=cc, yd=yd):
                send(xblk, rbuf.at[x, z, y], s_ry.at[i, cc], r_ry.at[y], x, fid(yd, z, cc))

    @pl.when(h == c)
    def _():
        rbuf[x, z, y] = right.astype(BF16)

    left_t = jnp.transpose(left)
    lsend[...] = left_t.astype(BF16)

    @pl.when(left_dst != f)
    def _():
        send(lsend, lb.at[x], s_lf.at[0], r_lf.at[0], x, left_dst)

    @pl.when(left_dst == f)
    def _():
        lb[x] = left_t.astype(BF16)

    @pl.when(gives_row)
    def _():
        send(
            lsend.at[pl.ds(pl.multiple_of(c * (BLK - 16), 16), 16)],
            rg.at[x], s_lf.at[1], r_lf.at[1], x, row_dst,
        )

    @pl.when(jnp.logical_not(has_row))
    def _():
        rg[x] = jnp.zeros((16, TOK), BF16)

    loads[0].wait()
    step_cells = 8 * dim

    @pl.loop(0, BLK // 8)
    def _(i):
        p2[pl.ds(i * 8 * nb, 8 * nb), :] = p1[pl.ds(i * step_cells, step_cells)].reshape(8 * nb, BLK)

    pair = lambda cc: pl.ds(half_y * cc, half_y)
    for yy in range(NY):

        @pl.when((yy != y) | (h != c))
        def _(yy=yy):
            arrive(rbuf.at[x, z, yy], r_ry.at[yy])

    def z_quad(r):
        out = []
        if r == 0:
            return [(0, z)]
        if r <= longs:
            out.append((2 * r - 1, zw(z - sig * r)))
        if r <= shorts:
            out.append((2 * r, zw(z + sig * r)))
        return out

    def round_a(r):
        for idx, zq in z_quad(r):
            ref = rbuf.at[x, zq, pair(c)]
            if r > 0:
                arrive(ref, r_rz.at[idx])
            is_long = r == 0 or idx % 2 == 1
            is_short = r == 0 or idx % 2 == 0
            if is_long and r < longs:
                send_later(ref, ref, s_rz.at[2 * r + 1], r_rz.at[2 * r + 1], x, z_long)
            if is_short and r < shorts:
                send_later(ref, ref, s_rz.at[2 * r + 2], r_rz.at[2 * r + 2], x, z_short)
            send_later(ref, ref, s_r1.at[idx, 0], r_r1.at[idx, 0], x_up, f)
            send_later(ref, ref, s_r1.at[idx, 1], r_r1.at[idx, 1], x_down, f)
            if r > 0:
                send_later(ref, ref, s_rp.at[x, zq], r_rp.at[x, zq], x, partner)

    def round_x1(r):
        for idx, zq in z_quad(r):
            for way, (frm, to) in enumerate(((x_down, x_up), (x_up, x_down))):
                ref = rbuf.at[frm, zq, pair(c)]
                arrive(ref, r_r1.at[idx, way])
                part = rbuf.at[frm, zq, half_y * c + way]
                send_later(part, part, s_r2.at[idx, way], r_r2.at[idx, way], to, f)
                send_later(ref, ref, s_rp.at[frm, zq], r_rp.at[frm, zq], x, partner)

    def round_x2(r):
        for idx, zq in z_quad(r):
            for way in range(2):
                arrive(rbuf.at[x_far, zq, half_y * c + way], r_r2.at[idx, way])
            ref = rbuf.at[x_far, zq, pair(c)]
            send_later(ref, ref, s_rp.at[x_far, zq], r_rp.at[x_far, zq], x, partner)

    round_a(0)

    @pl.when(left_src != f)
    def _():
        arrive(lb.at[x], r_lf.at[0])

    @pl.when(has_row)
    def _():
        arrive(rg.at[x], r_lf.at[1])

    for dx in range(1, NX):
        xx = (x + dx) % NX
        send_later(lb.at[x], lb.at[x], s_lx.at[dx - 1, 0], r_lx.at[x, 0], xx, f)
        send_later(rg.at[x], rg.at[x], s_lx.at[dx - 1, 1], r_lx.at[x, 1], xx, f)

    def build_left(xx):
        lt[pl.ds(0, 16), :] = rg[xx].astype(F32)
        lt[pl.ds(16, BLK), :] = lb[xx].astype(F32)
        lt[pl.ds(16 + BLK, 16), :] = rg[xx].astype(F32)
        before = lt[pl.ds(15, BLK), :]
        middle = lt[pl.ds(16, BLK), :]
        after = lt[pl.ds(17, BLK), :]
        zero = jnp.where(h == 0, middle, before)
        one = jnp.where(h == 0, after, middle)
        return zero, one

    zero, one = build_left(x)
    lown[:, pl.ds(0, BLK)] = jnp.transpose(zero).astype(BF16)
    lown[:, pl.ds(BLK, BLK)] = jnp.transpose(one).astype(BF16)

    tail_p = tails[pl.ds(0, 1), :]
    tail_here = jnp.where(par == 1, pltpu.roll(tails[...], 64, 1)[0:1], tail_p)

    def window_block(j):
        first = p2[pl.ds((j - m + nb) % nb, BLK, stride=nb), :]
        second = p2[pl.ds((j - m - 1 + nb) % nb, BLK, stride=nb), :]
        mixed = pltpu.roll(jnp.where(low, first, second), 64, 1)
        block = jnp.where(par == 1, mixed, first)
        column = j * BLK + lane
        carried = column < 64 * f
        top = jnp.where(carried, 0.0, block)
        bottom = jnp.where(carried, block, 0.0)
        is_tail = (row == BLK - 1) & (column >= 64 * f) & (column < 64 * f + 64)
        bottom = jnp.where(is_tail, tail_here, bottom)
        return jnp.concatenate([top, bottom], axis=0).astype(BF16)

    def partial_chunk(d):
        for mine in range(2):
            hh = c if mine == 0 else 1 - c
            wide = jnp.concatenate(
                [window_block((half_y * hh + i) * nz + d) for i in range(half_y)], axis=1
            )
            part = jnp.dot(lown[...], wide, preferred_element_type=F32)
            for i in range(half_y):
                target = pb if mine == 0 else xs
                target[d, i] = part[:, i * BLK : (i + 1) * BLK]
        send_later(xs.at[d], xr.at[d], s_sp.at[d], r_sp.at[d], x, partner)

    def round_c(r):
        if r >= longs:
            return
        partial_chunk(zw(z + sig * (longs - r)))
        partial_chunk(zw(z - sig * (shorts - r)))

    def chip_sum(d):
        arrive(xr.at[d], r_sp.at[d])
        return pb[d] + xr[d]

    def round_e(r):
        for way, (hops, to, sign) in enumerate(((longs, z_long, 1), (shorts, z_short, -1))):
            if r >= hops:
                continue
            d = zw(z + sig * sign * (hops - r))
            slot = 2 * r + way
            if r == 0:
                pb[d] = chip_sum(d)
                src = pb.at[d]
            else:
                before = slot - 2
                arrive(ring.at[before], r_sr.at[before])
                ring[before] = ring[before] + chip_sum(d)
                src = ring.at[before]
            send_later(src, ring.at[slot], s_sr.at[slot], r_sr.at[slot], x, to)

    def finish_sums():
        total = chip_sum(z)
        slot = 2 * (longs - 1)
        arrive(ring.at[slot], r_sr.at[slot])
        total = total + ring[slot]
        if shorts:
            slot = 2 * (shorts - 1) + 1
            arrive(ring.at[slot], r_sr.at[slot])
            total = total + ring[slot]
        pb[z] = total
        for i in range(half_y):
            for cc in range(CORES):
                yd = half_y * c + i

                @pl.when((yd != y) | (cc != c))
                def _(i=i, cc=cc, yd=yd):
                    send(pb.at[z, i], yb.at[y], s_sy.at[i, cc], r_sy.at[y], x, fid(yd, z, cc))

        @pl.when(h == c)
        def _():
            yb[y] = pb[z, y % half_y]

    def write_cotangents():
        for yy in range(NY):

            @pl.when((yy != y) | (h != c))
            def _(yy=yy):
                arrive(yb.at[yy], r_sy.at[yy])

        for out, base_y in ((gh_out, 0), (ga_out, half_y)):
            total = yb[base_y]
            for i in range(1, half_y):
                total = total + yb[base_y + i]
            total = jnp.where(c == 1, pltpu.roll(total, 64, 1), total)
            out[...] = total[:, :64].astype(BF16)

    def full_left():
        for xx in range(NX):

            @pl.when(xx != x)
            def _(xx=xx):
                arrive(lb.at[xx], r_lx.at[xx, 0])
                arrive(rg.at[xx], r_lx.at[xx, 1])

            zero, one = build_left(xx)
            ll[pl.ds(0, BLK), pl.ds(xx * TOK, TOK)] = zero.astype(BF16)
            ll[pl.ds(BLK, BLK), pl.ds(xx * TOK, TOK)] = one.astype(BF16)
        bias_own[...] = lax.dot_general(
            jnp.ones((8, NX * TOK), BF16), ll[pl.ds(0, BLK), :], NT, preferred_element_type=F32
        )
        me = z * CORES + c
        bias_grp[me] = bias_own[...]
        for i, (dz, dc) in enumerate(group):
            zz, cc = zw(z + dz), (c + dc) % CORES
            send_later(bias_own, bias_grp.at[me], s_bg.at[i], r_bg.at[me], x, fid(y, zz, cc))

    def bias_on():
        for dz, dc in group:
            other = zw(z + dz) * CORES + (c + dc) % CORES
            arrive(bias_grp.at[other], r_bg.at[other])
        send_later(bias_grp, bias_got, s_by, r_by, x, fid((y + 1) % NY, z, c))

    ext_ref[...] = jnp.zeros((8, BLK), F32)

    def gradient_quad(r):
        for _, zq in z_quad(r):
            for xx in range(NX):
                if r == 0:

                    @pl.when(xx != x)
                    def _(xx=xx, zq=zq):
                        arrive(rbuf.at[xx, zq, pair(1 - c)], r_rp.at[xx, zq])
                else:
                    arrive(rbuf.at[xx, zq, pair(1 - c)], r_rp.at[xx, zq])
            for yy in range(0, NY, 2):
                wide = jnp.concatenate(
                    [
                        jnp.concatenate([rbuf[xx, zq, yy], rbuf[xx, zq, yy + 1]], axis=1)
                        for xx in range(NX)
                    ],
                    axis=0,
                )
                both = jnp.dot(ll[...], wide, preferred_element_type=F32)
                for i in range(2):
                    j = (yy + i) * nz + zq
                    p_zero = both[:BLK, i * BLK : (i + 1) * BLK]
                    p_one = both[BLK:, i * BLK : (i + 1) * BLK]
                    bias = bias_got[j % (nb // 2)][0:1]
                    p_one = p_one + jnp.where((row == BLK - 1) & (f == nf // 2 - 1), bias, 0.0)
                    p_zero = p_zero + jnp.where((row == 0) & (f == nf // 2), bias, 0.0)
                    carried = j * BLK + lane < 64 * f
                    gw[j] = jnp.where(carried, p_one, p_zero)
                    ext_ref[...] = ext_ref[...] + jnp.where(
                        j == m, p_one[BLK - 8 :, :], jnp.zeros((8, BLK), F32)
                    )

    round_c(0)
    round_c(1)
    round_e(0)
    round_a(1)
    round_c(2)
    round_e(1)
    full_left()
    round_x1(0)
    round_a(2)
    round_c(3)
    round_e(2)
    bias_on()
    round_x1(1)
    round_x2(0)
    round_a(3)
    round_e(3)
    round_x1(2)
    round_x2(1)
    arrive(bias_got, r_by)
    gradient_quad(0)
    round_a(4)
    finish_sums()
    round_x1(3)
    round_x2(2)
    gradient_quad(1)
    round_x1(4)
    round_x2(3)
    gradient_quad(2)
    write_cotangents()
    round_x2(4)
    gradient_quad(3)
    gradient_quad(4)

    @pl.loop(0, nb)
    def _(b):
        first = gw[(b + m) % nb]
        second = gw[(b + m + 1) % nb]
        mixed = pltpu.roll(jnp.where(low, second, first), 64, 1)
        g2[pl.ds(b, BLK, stride=nb), :] = jnp.where(par == 1, mixed, first)

    one_scale = 1.0 / fixes[0]
    two_scale = 1.0 / fixes[1]

    def adam(grad, param, mom_one, mom_two):
        new_one = beta_one * mom_one + (1.0 - beta_one) * grad
        new_two = beta_two * mom_two + (1.0 - beta_two) * grad * grad
        direction = (new_one * one_scale) / (jnp.sqrt(new_two * two_scale) + adam_eps)
        return new_one, new_two, param - learn_rate * (direction + decay_rate * param)

    loads[1].wait()
    loads[2].wait()
    rows_each = 4
    span = rows_each * nb

    def adam_rows(i):
        at = pl.ds(pl.multiple_of(i * span, span), span)
        flat = pl.ds(pl.multiple_of(i * span * BLK, span * BLK), span * BLK)
        new_one, new_two, updated = adam(
            g2[at, :], p2[at, :], m1[flat].reshape(span, BLK), m2[flat].reshape(span, BLK)
        )
        o1[at, :] = new_one
        o2[at, :] = new_two
        p2[at, :] = updated
        return (updated * updated).reshape(rows_each, nb, BLK)

    acc_ref[...] = jnp.zeros((nb, BLK), F32)
    steps = BLK // rows_each

    @pl.loop(0, steps - 1)
    def _(i):
        acc_ref[...] = acc_ref[...] + jnp.sum(adam_rows(i), axis=0)

    squares = adam_rows(steps - 1)
    acc_main = acc_ref[...] + jnp.sum(squares[: rows_each - 1], axis=0)
    acc_last = squares[rows_each - 1]
    ext_row = ext_ref[...]
    ext_row = jnp.where(par == 1, pltpu.roll(ext_row, 64, 1), ext_row)[7:8]
    ext_one, ext_two, ext_up = adam(
        ext_row, tails[pl.ds(0, 1), :], tails[pl.ds(1, 1), :], tails[pl.ds(2, 1), :]
    )
    o1[pl.ds(nb * BLK, 8), :] = jnp.broadcast_to(ext_one, (8, BLK))
    o2[pl.ds(nb * BLK, 8), :] = jnp.broadcast_to(ext_two, (8, BLK))
    writes = [
        pltpu.make_async_copy(o1, n1_out, out_sem.at[0]),
        pltpu.make_async_copy(o2, n2_out, out_sem.at[1]),
    ]
    for write in writes:
        write.start()

    lane_row = lax.broadcasted_iota(jnp.int32, (1, BLK), 1)
    heads = lax.broadcasted_iota(jnp.int32, (nb, BLK), 1)
    blocks = lax.broadcasted_iota(jnp.int32, (nb, BLK), 0)
    low_b = heads < 64
    ext_sq = jnp.sum(jnp.where(lane_row < 64, ext_up * ext_up, 0.0), axis=1, keepdims=True)

    def head_of(part):
        spot = f + 2 * blocks + part
        carry = spot // nf
        by_column = (spot % nf) // 2
        main = jnp.where(h == 0, f, by_column)
        last_q = jnp.where(f + carry < nf // 2, f + carry, by_column)
        return main, last_q

    ext_head = jnp.where(f + 1 < nf // 2, f + 1, f // 2)
    total = jnp.where(lane_row == ext_head, ext_sq, 0.0)
    maps = [head_of(0), head_of(1)]
    for part in range(2):
        inside = low_b if part == 0 else jnp.logical_not(low_b)
        for which, acc in enumerate((acc_main, acc_last)):
            sums = jnp.sum(jnp.where(inside, acc, 0.0), axis=1, keepdims=True)
            total = total + jnp.sum(
                jnp.where(maps[part][which] == heads, sums, 0.0), axis=0, keepdims=True
            )
    s_own[...] = jnp.broadcast_to(total, (8, BLK))
    me = z * CORES + c
    s_grp[me] = s_own[...]
    for i, (dz, dc) in enumerate(group):
        zz, cc = zw(z + dz), (c + dc) % CORES
        send_later(s_own, s_grp.at[me], s_sg.at[i], r_sg.at[me], x, fid(y, zz, cc))
    for dz, dc in group:
        other = zw(z + dz) * CORES + (c + dc) % CORES
        arrive(s_grp.at[other], r_sg.at[other])
    s_mid[...] = jnp.sum(s_grp[...], axis=0)
    s_col[y] = s_mid[...]
    for dy in range(1, NY):
        yy = (y + dy) % NY
        send_later(s_mid, s_col.at[y], s_ss.at[dy - 1], r_ss.at[y], x, fid(yy, z, c))
    for dy in range(1, NY):
        yy = (y + dy) % NY
        arrive(s_col.at[yy], r_ss.at[yy])
    sumsq = jnp.sum(s_col[...], axis=0)[0:1]
    threshold = learn_rate * lasso_weight * math.sqrt(2 * HD * dim + HD)
    shrink = jnp.maximum(1.0 - threshold / jnp.sqrt(sumsq + norm_eps), 0.0)

    def factor(which):
        sides = [
            jnp.sum(jnp.where(maps[part][which] == heads, shrink, 0.0), axis=1, keepdims=True)
            for part in range(2)
        ]
        return jnp.where(low_b, sides[0], sides[1])

    acc_ref[...] = factor(0)
    last_ref[...] = factor(1)
    ext_shrink = jnp.sum(jnp.where(lane_row == ext_head, shrink, 0.0), axis=1, keepdims=True)

    @pl.loop(0, steps - 1)
    def _(i):
        at = pl.ds(pl.multiple_of(i * span, span), span)
        block = p2[at, :].reshape(rows_each, nb, BLK) * acc_ref[...][None]
        p2[at, :] = block.reshape(span, BLK)

    end = (steps - 1) * span
    at = pl.ds(end, span - nb)
    block = p2[at, :].reshape(rows_each - 1, nb, BLK) * acc_ref[...][None]
    p2[at, :] = block.reshape(span - nb, BLK)
    at = pl.ds(end + span - nb, nb)
    p2[at, :] = p2[at, :] * last_ref[...]
    p2[pl.ds(nb * BLK, 8), :] = jnp.broadcast_to(ext_up * ext_shrink, (8, BLK))
    final = pltpu.make_async_copy(p2, np_out, out_sem.at[2])
    final.start()

    for copy in pending:
        copy.wait_send()
    for i in range(half_y):
        for cc in range(CORES):
            yd = half_y * c + i

            @pl.when((yd != y) | (cc != c))
            def _(i=i, cc=cc, yd=yd):
                for src, ss in ((xblk, s_ry), (pb.at[z, i], s_sy)):
                    pltpu.make_async_remote_copy(
                        src_ref=src, dst_ref=src, send_sem=ss.at[i, cc], recv_sem=r_sw,
                        device_id=(x, partner), device_id_type=MESH,
                    ).wait_send()

    def sent(src, ss):
        pltpu.make_async_remote_copy(
            src_ref=src, dst_ref=src, send_sem=ss, recv_sem=r_sw,
            device_id=(x, partner), device_id_type=MESH,
        ).wait_send()

    @pl.when(left_dst != f)
    def _():
        sent(lsend, s_lf.at[0])

    @pl.when(gives_row)
    def _():
        sent(lsend.at[pl.ds(pl.multiple_of(c * (BLK - 16), 16), 16)], s_lf.at[1])

    for write in writes:
        write.wait()
    final.wait()


def on_device(
    nz, hidden, grad_query, attn_out, grad_output, flat_params, moment_one, moment_two, step_count
):
    nb = NY * nz
    cells = nb * BLK * BLK
    rows = nb * BLK
    shard_len = flat_params.shape[0]
    step_num = step_count[0].astype(F32)
    fixes = jnp.stack(
        [
            1.0 - jnp.power(jnp.float32(beta_one), step_num),
            1.0 - jnp.power(jnp.float32(beta_two), step_num),
        ]
    )
    tails = jnp.stack([flat_params[cells:], moment_one[cells:], moment_two[cells:]])
    tails = jnp.pad(tails, ((0, 5), (0, BLK - 64)))
    vm = lambda shape, dtype=F32: pltpu.VMEM(shape, dtype)
    dma = lambda *shape: pltpu.SemaphoreType.DMA(shape) if shape else pltpu.SemaphoreType.DMA
    grp = nz * CORES
    whole = pl.BlockSpec(memory_space=pltpu.VMEM)
    anywhere = pl.BlockSpec(memory_space=pl.ANY)
    scratch = [
        vm((cells,)), vm((cells,)), vm((cells,)),
        vm((rows + 8, BLK)), vm((rows + 8, BLK)), vm((rows + 8, BLK)), vm((rows, BLK)),
        vm((nb, BLK, BLK)),
        vm((TOK, BLK), BF16), vm((TOK, BLK), BF16), vm((TOK, BLK), BF16), vm((BLK, TOK), BF16),
        vm((NX, BLK, TOK), BF16), vm((NX, 16, TOK), BF16),
        vm((BLK + 32, TOK)), vm((2 * BLK, NX * TOK), BF16), vm((TOK, 2 * BLK), BF16),
        vm((NX, nz, NY, TOK, BLK), BF16),
        vm((nz, NY // 2, TOK, BLK)), vm((nz, NY // 2, TOK, BLK)), vm((nz, NY // 2, TOK, BLK)),
        vm((nz, NY // 2, TOK, BLK)), vm((NY, TOK, BLK)),
        vm((8, BLK)), vm((grp, 8, BLK)), vm((grp, 8, BLK)),
        vm((8, BLK)), vm((nb, BLK)), vm((nb, BLK)),
        vm((8, BLK)), vm((grp, 8, BLK)), vm((8, BLK)), vm((NY, 8, BLK)),
        dma(3), dma(3), dma(), dma(), dma(NY // 2, CORES), dma(NY), dma(2), dma(2),
        dma(NX - 1, 2), dma(NX, 2),
        dma(grp - 1), dma(grp), dma(), dma(), dma(nz), dma(nz), dma(nz, 2), dma(nz, 2),
        dma(nz, 2), dma(nz, 2), dma(NX, nz), dma(NX, nz),
        dma(nz), dma(nz), dma(nz), dma(nz), dma(NY // 2, CORES), dma(NY),
        dma(grp - 1), dma(grp), dma(NY - 1), dma(NY),
    ]
    outs = pl.pallas_call(
        functools.partial(kernel, nz),
        out_shape=[
            jax.ShapeDtypeStruct((TOK, 64), BF16),
            jax.ShapeDtypeStruct((TOK, 64), BF16),
            jax.ShapeDtypeStruct((rows + 8, BLK), F32),
            jax.ShapeDtypeStruct((rows + 8, BLK), F32),
            jax.ShapeDtypeStruct((rows + 8, BLK), F32),
        ],
        in_specs=[whole] * 5 + [pl.BlockSpec(memory_space=pltpu.SMEM)] + [anywhere] * 3,
        out_specs=[whole] * 2 + [anywhere] * 3,
        scratch_shapes=scratch,
        compiler_params=pltpu.CompilerParams(
            collective_id=0, has_side_effects=True, vmem_limit_bytes=48 * 1024 * 1024
        ),
        cost_estimate=pl.CostEstimate(
            flops=4 * 512 * 128 * 4096, bytes_accessed=6 * 2 * 1024 * 1024, transcendentals=524352
        ),
        name="step",
    )(
        hidden, grad_query, attn_out, grad_output, tails, fixes,
        flat_params, moment_one, moment_two,
    )
    grad_hidden, grad_attn = outs[:2]
    new_params, new_one, new_two = (part.reshape(-1)[:shard_len] for part in outs[2:])
    return (grad_hidden, grad_attn, new_params, new_one, new_two)


def solution(mesh):
    nz = mesh.shape["fsdp"] // (NY * CORES)
    in_specs = (
        P("dp", "fsdp"),
        P("dp", "fsdp"),
        P("dp", "fsdp"),
        P("dp", "fsdp"),
        P("fsdp"),
        P("fsdp"),
        P("fsdp"),
        P(),
    )
    out_specs = (P("dp", "fsdp"), P("dp", "fsdp"), P("fsdp"), P("fsdp"), P("fsdp"))
    return jax.shard_map(
        functools.partial(on_device, nz), mesh=mesh, in_specs=in_specs, out_specs=out_specs, check_vma=False
    )
```

```python
import functools
import math

import jax
import jax.numpy as jnp
from jax import lax
from jax.experimental import pallas as pl
from jax.experimental.pallas import tpu as pltpu
from jax.sharding import PartitionSpec as P

HD = 128
NX = 4
NY = 4
CORES = 2
TOK = 128
BLK = 128

beta_one = 0.9
beta_two = 0.95
adam_eps = 1e-08
learn_rate = 0.02
decay_rate = 0.1
lasso_weight = 2.0
norm_eps = 1e-06

MESH = pl.DeviceIdType.MESH
F32 = jnp.float32
BF16 = jnp.bfloat16
NT = (((1,), (1,)), ((), ()))


def kernel(
    nz, acts, p_tail, m1_tail, m2_tail, fixes, p_hbm, m1_hbm, m2_hbm,
    gh_out, ga_out, up_out, n1_out, n2_out, factor_out,
    p1, m1, m2, p2, o1, o2, g2, gw,
    lb, rg, lt, ll, lown,
    rbuf, pb, xs, xr, ring, yb, bias_own, bias_grp, bias_got,
    ext_ref, acc_ref, s_own, s_grp,
    in_sem, out_sem, self_sem, s_ry, r_ry, s_lf, r_lf, s_lx, r_lx,
    s_bg, r_bg, s_by, r_by, s_rz, r_rz, s_r1, r_r1, s_r2, r_r2, s_rp, r_rp,
    s_sp, r_sp, s_sr, r_sr, s_sy, r_sy, s_sg, r_sg,
):
    h_in, gq_in, a_in, go_in = (acts.at[i] for i in range(4))
    nf = NY * nz * CORES
    nb = NY * nz
    dim = nb * BLK
    half_y = NY // 2
    longs, shorts = nz // 2, nz - 1 - nz // 2
    x = lax.axis_index("dp")
    f = lax.axis_index("fsdp")
    c = f % CORES
    z = (f // CORES) % nz
    y = f // (CORES * nz)
    h = y // half_y
    m = f // 2
    par = f % 2
    k = f // CORES
    sig = 1 - 2 * c

    def fid(yy, zz, cc):
        return (yy * nz + zz) * CORES + cc

    def zw(v):
        return (v + 2 * nz) % nz

    partner = fid(y, z, 1 - c)
    z_long = fid(y, zw(z + sig), c)
    z_short = fid(y, zw(z - sig), c)
    x_up = (x + 1) % NX
    x_down = (x + NX - 1) % NX
    x_far = (x + 2) % NX

    pending = []

    def send(src, dst, ss, rs, xx, ff):
        copy = pltpu.make_async_remote_copy(
            src_ref=src, dst_ref=dst, send_sem=ss, recv_sem=rs,
            device_id=(xx, ff), device_id_type=MESH,
        )
        copy.start()
        return copy

    def send_later(*args):
        pending.append(send(*args))

    def arrive(dst, rs):
        pltpu.make_async_remote_copy(
            src_ref=dst, dst_ref=dst, send_sem=s_by, recv_sem=rs,
            device_id=(x, partner), device_id_type=MESH,
        ).wait_recv()

    cells = nb * BLK * BLK
    loads = [
        pltpu.make_async_copy(src.at[pl.ds(0, cells)], dst, in_sem.at[i])
        for i, (src, dst) in enumerate(((p_hbm, p1), (m1_hbm, m1), (m2_hbm, m2)))
    ]
    for load in loads:
        load.start()

    barrier = pltpu.get_barrier_semaphore()

    def greet(xx, ff):
        pl.semaphore_signal(barrier, inc=1, device_id=(xx, ff), device_id_type=MESH)

    group = [(dz, dc) for dz in range(nz) for dc in range(CORES) if (dz, dc) != (0, 0)]
    for dz, dc in group:
        greet(x, fid(y, zw(z + dz), (c + dc) % CORES))
    for dy in range(1, NY):
        for dc in range(CORES):
            greet(x, fid((y + dy) % NY, z, (c + dc) % CORES))
    for dx in range(1, NX):
        greet((x + dx) % NX, f)
    fl = f % (nf // 2)
    row_src = 2 * (fl + 1 - 2 * h) + h
    row_chip = fl + 1 - 2 * h
    has_row = (row_chip >= 0) & (row_chip < nf // 2)
    left_dsts = (k, nf // 2 + k)
    left_srcs = (2 * fl, 2 * fl + 1)
    row_dst_low = k - 1 + 2 * c
    gives_row = (row_dst_low >= 0) & (row_dst_low < nf // 2)
    row_dst = c * (nf // 2) + row_dst_low

    for src in left_srcs:

        @pl.when(src != f)
        def _(src=src):
            greet(x, src)

    @pl.when(has_row)
    def _():
        greet(x, row_src)

    greeted = len(group) + (NY - 1) * CORES + NX - 1
    for dst in left_dsts:
        greeted = greeted + (dst != f).astype(jnp.int32)
    greeted = greeted + gives_row.astype(jnp.int32)
    pl.semaphore_wait(barrier, greeted)

    lane = lax.broadcasted_iota(jnp.int32, (BLK, BLK), 1)
    row = lax.broadcasted_iota(jnp.int32, (BLK, BLK), 0)
    low = lane < 64
    own_half = pl.ds(pl.multiple_of(c * 64, 64), 64)

    def right_sends():
        for yd in range(NY):
            src = h_in if yd < half_y else a_in
            for cc in range(CORES):
                yield yd, cc, src

    for yd, cc, src in right_sends():
        remote = (yd != y) | (cc != c)

        @pl.when(remote)
        def _(yd=yd, cc=cc, src=src):
            send(
                src, rbuf.at[x, z, y, own_half], s_ry.at[yd, cc], r_ry.at[y, c], x, fid(yd, z, cc)
            )

        @pl.when(jnp.logical_not(remote))
        def _(src=src):
            pltpu.make_async_copy(src, rbuf.at[x, z, y, own_half], self_sem.at[0]).start()

    row_part = lambda src: src.at[pl.ds(pl.multiple_of(c * (64 - 16), 16), 16)]
    for i, (src, dst) in enumerate(zip((gq_in, go_in), left_dsts)):

        @pl.when(dst != f)
        def _(i=i, src=src, dst=dst):
            send(src, lb.at[x, own_half], s_lf.at[i], r_lf.at[c], x, dst)

        @pl.when(dst == f)
        def _(src=src):
            pltpu.make_async_copy(src, lb.at[x, own_half], self_sem.at[1]).start()

        @pl.when(gives_row & (c == i))
        def _(src=src):
            send(row_part(src), rg.at[x], s_lf.at[2], r_lf.at[2], x, row_dst)

    @pl.when(jnp.logical_not(has_row))
    def _():
        rg[x] = jnp.zeros((16, TOK), BF16)

    loads[0].wait()
    step_cells = 8 * dim

    @pl.loop(0, BLK // 8)
    def _(i):
        p2[pl.ds(i * 8 * nb, 8 * nb), :] = p1[pl.ds(i * step_cells, step_cells)].reshape(8 * nb, BLK)

    pair = lambda cc: pl.ds(half_y * cc, half_y)
    def own_quad():
        for yy in range(NY):
            for cc in range(CORES):
                remote = (yy != y) | (cc != c)
                half = rbuf.at[x, z, yy, pl.ds(cc * 64, 64)]

                @pl.when(remote)
                def _(yy=yy, cc=cc, half=half):
                    arrive(half, r_ry.at[yy, cc])

        pltpu.make_async_copy(h_in, rbuf.at[x, z, y, own_half], self_sem.at[0]).wait()

    def z_quad(r):
        out = []
        if r == 0:
            return [(0, z)]
        if r <= longs:
            out.append((2 * r - 1, zw(z - sig * r)))
        if r <= shorts:
            out.append((2 * r, zw(z + sig * r)))
        return out

    def round_a(r):
        for idx, zq in z_quad(r):
            ref = rbuf.at[x, zq, pair(c)]
            if r > 0:
                arrive(ref, r_rz.at[idx])
            is_long = r == 0 or idx % 2 == 1
            is_short = r == 0 or idx % 2 == 0
            if is_long and r < longs:
                send_later(ref, ref, s_rz.at[2 * r + 1], r_rz.at[2 * r + 1], x, z_long)
            if is_short and r < shorts:
                send_later(ref, ref, s_rz.at[2 * r + 2], r_rz.at[2 * r + 2], x, z_short)
            send_later(ref, ref, s_r1.at[idx, 0], r_r1.at[idx, 0], x_up, f)
            send_later(ref, ref, s_r1.at[idx, 1], r_r1.at[idx, 1], x_down, f)
            if r > 0:
                send_later(ref, ref, s_rp.at[x, zq], r_rp.at[x, zq], x, partner)

    def round_x1(r):
        for idx, zq in z_quad(r):
            for way, (frm, to) in enumerate(((x_down, x_up), (x_up, x_down))):
                ref = rbuf.at[frm, zq, pair(c)]
                arrive(ref, r_r1.at[idx, way])
                part = rbuf.at[frm, zq, half_y * c + way]
                send_later(part, part, s_r2.at[idx, way], r_r2.at[idx, way], to, f)
                send_later(ref, ref, s_rp.at[frm, zq], r_rp.at[frm, zq], x, partner)

    def round_x2(r):
        for idx, zq in z_quad(r):
            for way in range(2):
                arrive(rbuf.at[x_far, zq, half_y * c + way], r_r2.at[idx, way])
            ref = rbuf.at[x_far, zq, pair(c)]
            send_later(ref, ref, s_rp.at[x_far, zq], r_rp.at[x_far, zq], x, partner)

    own_quad()
    round_a(0)

    for cc, src in enumerate(left_srcs):

        @pl.when(src != f)
        def _(cc=cc):
            arrive(lb.at[x, pl.ds(cc * 64, 64)], r_lf.at[cc])

        @pl.when(src == f)
        def _():
            pltpu.make_async_copy(gq_in, lb.at[x, own_half], self_sem.at[1]).wait()

    @pl.when(has_row)
    def _():
        arrive(rg.at[x], r_lf.at[2])

    for dx in range(1, NX):
        xx = (x + dx) % NX
        send_later(lb.at[x], lb.at[x], s_lx.at[dx - 1, 0], r_lx.at[x, 0], xx, f)
        send_later(rg.at[x], rg.at[x], s_lx.at[dx - 1, 1], r_lx.at[x, 1], xx, f)

    def build_left(xx):
        lt[pl.ds(0, 16), :] = rg[xx].astype(F32)
        lt[pl.ds(16, BLK), :] = lb[xx].astype(F32)
        lt[pl.ds(16 + BLK, 16), :] = rg[xx].astype(F32)
        before = lt[pl.ds(15, BLK), :]
        middle = lt[pl.ds(16, BLK), :]
        after = lt[pl.ds(17, BLK), :]
        zero = jnp.where(h == 0, middle, before)
        one = jnp.where(h == 0, after, middle)
        return zero, one

    zero, one = build_left(x)
    lown[:, pl.ds(0, BLK)] = jnp.transpose(zero).astype(BF16)
    lown[:, pl.ds(BLK, BLK)] = jnp.transpose(one).astype(BF16)

    lane_row = lax.broadcasted_iota(jnp.int32, (1, BLK), 1)

    def tail_row(ref):
        return jnp.where(lane_row < 64, ref[...].reshape(8, BLK)[0:1], 0.0)

    tail_p = tail_row(p_tail)
    tail_here = jnp.where(
        par == 1, pltpu.roll(jnp.broadcast_to(tail_p, (8, BLK)), 64, 1)[0:1], tail_p
    )

    def window_block(j):
        first = p2[pl.ds((j - m + nb) % nb, BLK, stride=nb), :]
        second = p2[pl.ds((j - m - 1 + nb) % nb, BLK, stride=nb), :]
        mixed = pltpu.roll(jnp.where(low, first, second), 64, 1)
        block = jnp.where(par == 1, mixed, first)
        column = j * BLK + lane
        carried = column < 64 * f
        top = jnp.where(carried, 0.0, block)
        bottom = jnp.where(carried, block, 0.0)
        is_tail = (row == BLK - 1) & (column >= 64 * f) & (column < 64 * f + 64)
        bottom = jnp.where(is_tail, tail_here, bottom)
        return jnp.concatenate([top, bottom], axis=0).astype(BF16)

    def partial_chunk(d):
        for mine in range(2):
            hh = c if mine == 0 else 1 - c
            wide = jnp.concatenate(
                [window_block((half_y * hh + i) * nz + d) for i in range(half_y)], axis=1
            )
            part = jnp.dot(lown[...], wide, preferred_element_type=F32)
            for i in range(half_y):
                target = pb if mine == 0 else xs
                target[d, i] = part[:, i * BLK : (i + 1) * BLK]
        send_later(xs.at[d], xr.at[d], s_sp.at[d], r_sp.at[d], x, partner)

    def round_c(r):
        if r >= longs:
            return
        partial_chunk(zw(z + sig * (longs - r)))
        partial_chunk(zw(z - sig * (shorts - r)))

    def chip_sum(d):
        arrive(xr.at[d], r_sp.at[d])
        return pb[d] + xr[d]

    def round_e(r):
        for way, (hops, to, sign) in enumerate(((longs, z_long, 1), (shorts, z_short, -1))):
            if r >= hops:
                continue
            d = zw(z + sig * sign * (hops - r))
            slot = 2 * r + way
            if r == 0:
                pb[d] = chip_sum(d)
                src = pb.at[d]
            else:
                before = slot - 2
                arrive(ring.at[before], r_sr.at[before])
                ring[before] = ring[before] + chip_sum(d)
                src = ring.at[before]
            send_later(src, ring.at[slot], s_sr.at[slot], r_sr.at[slot], x, to)

    def finish_sums():
        total = chip_sum(z)
        slot = 2 * (longs - 1)
        arrive(ring.at[slot], r_sr.at[slot])
        total = total + ring[slot]
        if shorts:
            slot = 2 * (shorts - 1) + 1
            arrive(ring.at[slot], r_sr.at[slot])
            total = total + ring[slot]
        pb[z] = total
        for i in range(half_y):
            for cc in range(CORES):
                yd = half_y * c + i

                @pl.when((yd != y) | (cc != c))
                def _(i=i, cc=cc, yd=yd):
                    send(pb.at[z, i], yb.at[y], s_sy.at[i, cc], r_sy.at[y], x, fid(yd, z, cc))

        @pl.when(h == c)
        def _():
            yb[y] = pb[z, y % half_y]

    def write_cotangents():
        for yy in range(NY):

            @pl.when((yy != y) | (h != c))
            def _(yy=yy):
                arrive(yb.at[yy], r_sy.at[yy])

        for out, base_y in ((gh_out, 0), (ga_out, half_y)):
            total = yb[base_y]
            for i in range(1, half_y):
                total = total + yb[base_y + i]
            total = jnp.transpose(total)
            out[...] = jnp.where(c == 1, total[64:], total[:64]).astype(BF16)

    def full_left():
        for xx in range(NX):

            @pl.when(xx != x)
            def _(xx=xx):
                arrive(lb.at[xx], r_lx.at[xx, 0])
                arrive(rg.at[xx], r_lx.at[xx, 1])

            zero, one = build_left(xx)
            ll[pl.ds(0, BLK), pl.ds(xx * TOK, TOK)] = zero.astype(BF16)
            ll[pl.ds(BLK, BLK), pl.ds(xx * TOK, TOK)] = one.astype(BF16)
        bias_own[...] = lax.dot_general(
            jnp.ones((8, NX * TOK), BF16), ll[pl.ds(0, BLK), :], NT, preferred_element_type=F32
        )
        me = z * CORES + c
        bias_grp[me] = bias_own[...]
        for i, (dz, dc) in enumerate(group):
            zz, cc = zw(z + dz), (c + dc) % CORES
            send_later(bias_own, bias_grp.at[me], s_bg.at[i], r_bg.at[me], x, fid(y, zz, cc))

    def bias_on():
        for dz, dc in group:
            other = zw(z + dz) * CORES + (c + dc) % CORES
            arrive(bias_grp.at[other], r_bg.at[other])
        send_later(bias_grp, bias_got, s_by, r_by, x, fid((y + 1) % NY, z, c))

    ext_ref[...] = jnp.zeros((8, BLK), F32)

    def gradient_quad(r):
        for _, zq in z_quad(r):
            for xx in range(NX):
                if r == 0:

                    @pl.when(xx != x)
                    def _(xx=xx, zq=zq):
                        arrive(rbuf.at[xx, zq, pair(1 - c)], r_rp.at[xx, zq])
                else:
                    arrive(rbuf.at[xx, zq, pair(1 - c)], r_rp.at[xx, zq])
            for yy in range(0, NY, 2):
                wide = jnp.concatenate(
                    [
                        jnp.concatenate([rbuf[xx, zq, yy], rbuf[xx, zq, yy + 1]], axis=0)
                        for xx in range(NX)
                    ],
                    axis=1,
                )
                both = lax.dot_general(ll[...], wide, NT, preferred_element_type=F32)
                for i in range(2):
                    j = (yy + i) * nz + zq
                    p_zero = both[:BLK, i * BLK : (i + 1) * BLK]
                    p_one = both[BLK:, i * BLK : (i + 1) * BLK]
                    bias = bias_got[j % (nb // 2)][0:1]
                    p_one = p_one + jnp.where((row == BLK - 1) & (f == nf // 2 - 1), bias, 0.0)
                    p_zero = p_zero + jnp.where((row == 0) & (f == nf // 2), bias, 0.0)
                    carried = j * BLK + lane < 64 * f
                    gw[j] = jnp.where(carried, p_one, p_zero)
                    ext_ref[...] = ext_ref[...] + jnp.where(
                        j == m, p_one[BLK - 8 :, :], jnp.zeros((8, BLK), F32)
                    )

    def reorder(zc):
        for yy in range(NY):
            j = yy * nz + zc
            first = gw[j]
            second = gw[(j + 1) % nb]
            mixed = pltpu.roll(jnp.where(low, second, first), 64, 1)
            g2[pl.ds((j - m + nb) % nb, BLK, stride=nb), :] = jnp.where(par == 1, mixed, first)

    def gradient(r):
        gradient_quad(r)
        if 0 < r <= longs:
            reorder(zw(z - r))
            reorder(zw(z + r - 1))

    round_c(0)
    round_c(1)
    round_a(1)
    round_e(0)
    round_c(2)
    round_x1(0)
    full_left()
    round_a(2)
    round_c(3)
    round_x1(1)
    round_x2(0)
    round_e(1)
    bias_on()
    round_a(3)
    round_x1(2)
    round_x2(1)
    round_e(2)
    round_a(4)
    round_x1(3)
    round_x2(2)
    arrive(bias_got, r_by)
    gradient(0)
    round_e(3)
    round_x1(4)
    round_x2(3)
    gradient(1)
    gradient(2)
    round_x2(4)
    gradient(3)
    gradient(4)

    one_scale = 1.0 / fixes[0]
    two_scale = 1.0 / fixes[1]

    def adam(grad, param, mom_one, mom_two):
        new_one = beta_one * mom_one + (1.0 - beta_one) * grad
        new_two = beta_two * mom_two + (1.0 - beta_two) * grad * grad
        direction = (new_one * one_scale) / (jnp.sqrt(new_two * two_scale) + adam_eps)
        return new_one, new_two, param - learn_rate * (direction + decay_rate * param)

    loads[1].wait()
    loads[2].wait()
    rows_each = 4
    span = rows_each * nb

    def adam_rows(i):
        at = pl.ds(pl.multiple_of(i * span, span), span)
        flat = pl.ds(pl.multiple_of(i * span * BLK, span * BLK), span * BLK)
        new_one, new_two, updated = adam(
            g2[at, :], p2[at, :], m1[flat].reshape(span, BLK), m2[flat].reshape(span, BLK)
        )
        o1[at, :] = new_one
        o2[at, :] = new_two
        p2[at, :] = updated
        return (updated * updated).reshape(rows_each, nb, BLK)

    acc_ref[...] = jnp.zeros((nb, BLK), F32)
    steps = BLK // rows_each

    @pl.loop(0, steps - 1)
    def _(i):
        acc_ref[...] = acc_ref[...] + jnp.sum(adam_rows(i), axis=0)

    squares = adam_rows(steps - 1)
    acc_main = acc_ref[...] + jnp.sum(squares[: rows_each - 1], axis=0)
    acc_last = squares[rows_each - 1]
    ext_row = ext_ref[...]
    ext_row = jnp.where(par == 1, pltpu.roll(ext_row, 64, 1), ext_row)[7:8]
    ext_one, ext_two, ext_up = adam(
        ext_row, tail_p, tail_row(m1_tail), tail_row(m2_tail)
    )
    o1[pl.ds(nb * BLK, 8), :] = jnp.broadcast_to(ext_one, (8, BLK))
    o2[pl.ds(nb * BLK, 8), :] = jnp.broadcast_to(ext_two, (8, BLK))
    p2[pl.ds(nb * BLK, 8), :] = jnp.broadcast_to(ext_up, (8, BLK))
    writes = [
        pltpu.make_async_copy(p2, up_out, out_sem.at[2]),
        pltpu.make_async_copy(o1, n1_out, out_sem.at[0]),
        pltpu.make_async_copy(o2, n2_out, out_sem.at[1]),
    ]
    for write in writes:
        write.start()

    heads = lax.broadcasted_iota(jnp.int32, (nb, BLK), 1)
    blocks = lax.broadcasted_iota(jnp.int32, (nb, BLK), 0)
    low_b = heads < 64
    ext_sq = jnp.sum(jnp.where(lane_row < 64, ext_up * ext_up, 0.0), axis=1, keepdims=True)

    def head_of(part):
        spot = f + 2 * blocks + part
        carry = spot // nf
        by_column = (spot % nf) // 2
        main = jnp.where(h == 0, f, by_column)
        last_q = jnp.where(f + carry < nf // 2, f + carry, by_column)
        return main, last_q

    ext_head = jnp.where(f + 1 < nf // 2, f + 1, f // 2)
    total = jnp.where(lane_row == ext_head, ext_sq, 0.0)
    maps = [head_of(0), head_of(1)]
    for part in range(2):
        inside = low_b if part == 0 else jnp.logical_not(low_b)
        for which, acc in enumerate((acc_main, acc_last)):
            sums = jnp.sum(jnp.where(inside, acc, 0.0), axis=1, keepdims=True)
            total = total + jnp.sum(
                jnp.where(maps[part][which] == heads, sums, 0.0), axis=0, keepdims=True
            )
    s_own[...] = total
    offsets = [
        (dy, dz, dc)
        for dy in range(NY)
        for dz in range(nz)
        for dc in range(CORES)
        if (dy, dz, dc) != (0, 0, 0)
    ]
    offsets.sort(key=lambda o: -(min(o[0], NY - o[0]) + min(o[1], nz - o[1])))
    for i, (dy, dz, dc) in enumerate(offsets):
        target = fid((y + dy) % NY, zw(z + dz), (c + dc) % CORES)
        send(s_own, s_grp.at[i], s_sg, r_sg, x, target)
    finish_sums()
    arrive(s_grp, r_sg)
    sumsq = s_own[...] + jnp.sum(s_grp[...], axis=0)
    threshold = learn_rate * lasso_weight * math.sqrt(2 * HD * dim + HD)
    shrink = jnp.maximum(1.0 - threshold / jnp.sqrt(sumsq + norm_eps), 0.0)

    def factor(which):
        sides = [
            jnp.sum(jnp.where(maps[part][which] == heads, shrink, 0.0), axis=1, keepdims=True)
            for part in range(2)
        ]
        return jnp.where(low_b, sides[0], sides[1])

    factor_out[pl.ds(0, nb), :] = factor(0)
    factor_out[pl.ds(nb, nb), :] = factor(1)
    ext_shrink = jnp.sum(jnp.where(lane_row == ext_head, shrink, 0.0), axis=1, keepdims=True)
    factor_out[pl.ds(2 * nb, 8), :] = jnp.broadcast_to(ext_shrink, (8, BLK))

    write_cotangents()

    def sent(src, ss):
        pltpu.make_async_remote_copy(
            src_ref=src, dst_ref=src, send_sem=ss, recv_sem=r_by,
            device_id=(x, partner), device_id_type=MESH,
        ).wait_send()

    sent(s_grp, s_sg)
    for copy in pending:
        copy.wait_send()
    for yd, cc, src in right_sends():

        @pl.when((yd != y) | (cc != c))
        def _(yd=yd, cc=cc, src=src):
            sent(src, s_ry.at[yd, cc])

    for i in range(half_y):
        for cc in range(CORES):
            yd = half_y * c + i

            @pl.when((yd != y) | (cc != c))
            def _(i=i, cc=cc):
                sent(pb.at[z, i], s_sy.at[i, cc])

    for i, (src, dst) in enumerate(zip((gq_in, go_in), left_dsts)):

        @pl.when(dst != f)
        def _(i=i, src=src):
            sent(src, s_lf.at[i])

    @pl.when(gives_row)
    def _():
        sent(row_part(gq_in), s_lf.at[2])

    for write in writes:
        write.wait()


def finish(nb, gh, ga, up, n1, n2, factors, gh_out, ga_out, np_out, n1_out, n2_out, scaled, sems):
    copies = [
        pltpu.make_async_copy(gh, gh_out, sems.at[6]),
        pltpu.make_async_copy(ga, ga_out, sems.at[7]),
        pltpu.make_async_copy(n1, n1_out, sems.at[0]),
        pltpu.make_async_copy(n2, n2_out, sems.at[1]),
    ]
    for copy in copies:
        copy.start()
    pieces, rows_each = 4, 4
    span = rows_each * nb
    steps = BLK // rows_each // pieces
    main = factors[pl.ds(0, nb), :]
    for piece in range(pieces):
        start = piece * steps * span
        full = steps - 1 if piece == pieces - 1 else steps

        @pl.loop(0, full)
        def _(i):
            at = pl.ds(pl.multiple_of(start + i * span, span), span)
            block = up[at, :].reshape(rows_each, nb, BLK) * factors[pl.ds(0, nb), :][None]
            scaled[at, :] = block.reshape(span, BLK)

        rows = steps * span
        if piece == pieces - 1:
            at = pl.ds(start + full * span, span - nb)
            block = up[at, :].reshape(rows_each - 1, nb, BLK) * main[None]
            scaled[at, :] = block.reshape(span - nb, BLK)
            at = pl.ds(nb * BLK - nb, nb)
            scaled[at, :] = up[at, :] * factors[pl.ds(nb, nb), :]
            at = pl.ds(nb * BLK, 8)
            scaled[at, :] = up[at, :] * factors[pl.ds(2 * nb, 8), :]
            rows += 8
        at = pl.ds(start, rows)
        copy = pltpu.make_async_copy(scaled.at[at], np_out.at[at], sems.at[2 + piece])
        copy.start()
        copies.append(copy)
    for copy in copies:
        copy.wait()


def on_device(
    nz, hidden, grad_query, attn_out, grad_output, flat_params, moment_one, moment_two, step_count
):
    nb = NY * nz
    cells = nb * BLK * BLK
    rows = nb * BLK
    shard_len = flat_params.shape[0]
    step_num = step_count[0].astype(F32)
    fixes = jnp.stack(
        [
            1.0 - jnp.power(jnp.float32(beta_one), step_num),
            1.0 - jnp.power(jnp.float32(beta_two), step_num),
        ]
    )
    vm = lambda shape, dtype=F32: pltpu.VMEM(shape, dtype)
    dma = lambda *shape: pltpu.SemaphoreType.DMA(shape) if shape else pltpu.SemaphoreType.DMA
    grp = nz * CORES
    whole = pl.BlockSpec(memory_space=pltpu.VMEM)
    anywhere = pl.BlockSpec(memory_space=pl.ANY)
    scratch = [
        vm((cells,)), vm((cells,)), vm((cells,)),
        vm((rows + 8, BLK)), vm((rows + 8, BLK)), vm((rows + 8, BLK)), vm((rows, BLK)),
        vm((nb, BLK, BLK)),
        vm((NX, BLK, TOK), BF16), vm((NX, 16, TOK), BF16),
        vm((BLK + 32, TOK)), vm((2 * BLK, NX * TOK), BF16), vm((TOK, 2 * BLK), BF16),
        vm((NX, nz, NY, TOK, BLK), BF16),
        vm((nz, NY // 2, TOK, BLK)), vm((nz, NY // 2, TOK, BLK)), vm((nz, NY // 2, TOK, BLK)),
        vm((nz, NY // 2, TOK, BLK)), vm((NY, TOK, BLK)),
        vm((8, BLK)), vm((grp, 8, BLK)), vm((grp, 8, BLK)),
        vm((8, BLK)), vm((nb, BLK)),
        vm((1, BLK)), vm((NY * grp - 1, 1, BLK)),
        dma(3), dma(3), dma(2), dma(NY, CORES), dma(NY, CORES), dma(3), dma(3),
        dma(NX - 1, 2), dma(NX, 2),
        dma(grp - 1), dma(grp), dma(), dma(), dma(nz), dma(nz), dma(nz, 2), dma(nz, 2),
        dma(nz, 2), dma(nz, 2), dma(NX, nz), dma(NX, nz),
        dma(nz), dma(nz), dma(nz), dma(nz), dma(NY // 2, CORES), dma(NY),
        dma(), dma(),
    ]
    cotangent = jax.ShapeDtypeStruct((64, TOK), BF16)
    flat = jax.ShapeDtypeStruct((rows + 8, BLK), F32)
    tail = pl.BlockSpec((1024,), lambda i: (cells // 1024,))
    outs = pl.pallas_call(
        functools.partial(kernel, nz),
        grid=(1,),
        out_shape=[
            cotangent, cotangent,
            flat, flat, flat,
            jax.ShapeDtypeStruct((2 * nb + 8, BLK), F32),
        ],
        in_specs=[anywhere] + [tail] * 3 + [pl.BlockSpec(memory_space=pltpu.SMEM)] + [anywhere] * 3,
        out_specs=[whole] * 2 + [anywhere] * 3 + [whole],
        scratch_shapes=scratch,
        compiler_params=pltpu.CompilerParams(
            collective_id=0, has_side_effects=True, vmem_limit_bytes=46 * 1024 * 1024
        ),
        cost_estimate=pl.CostEstimate(
            flops=4 * 512 * 128 * 4096, bytes_accessed=6 * 2 * 1024 * 1024, transcendentals=524352
        ),
        name="step",
    )(
        jnp.stack([hidden.T, grad_query.T, attn_out.T, grad_output.T]),
        flat_params, moment_one, moment_two, fixes, flat_params, moment_one, moment_two,
    )
    results = pl.pallas_call(
        functools.partial(finish, nb),
        out_shape=[cotangent] * 2 + [flat] * 3,
        in_specs=[anywhere, anywhere, whole, anywhere, anywhere, whole],
        out_specs=[anywhere] * 5,
        scratch_shapes=[vm((rows + 8, BLK)), dma(8)],
        compiler_params=pltpu.CompilerParams(vmem_limit_bytes=16 * 1024 * 1024),
        name="finish",
    )(*outs)
    grad_hidden, grad_attn = results[0].T, results[1].T
    new_params, new_one, new_two = (part.reshape(-1)[:shard_len] for part in results[2:])
    return (grad_hidden, grad_attn, new_params, new_one, new_two)


def solution(mesh):
    nz = mesh.shape["fsdp"] // (NY * CORES)
    in_specs = (
        P("dp", "fsdp"),
        P("dp", "fsdp"),
        P("dp", "fsdp"),
        P("dp", "fsdp"),
        P("fsdp"),
        P("fsdp"),
        P("fsdp"),
        P(),
    )
    out_specs = (P("dp", "fsdp"), P("dp", "fsdp"), P("fsdp"), P("fsdp"), P("fsdp"))
    return jax.shard_map(
        functools.partial(on_device, nz), mesh=mesh, in_specs=in_specs, out_specs=out_specs, check_vma=False
    )
```

```python
import functools
import math

import jax
import jax.numpy as jnp
from jax import lax
from jax.experimental import pallas as pl
from jax.experimental.pallas import tpu as pltpu
from jax.sharding import PartitionSpec as P

HD = 128
NX = 4
NY = 4
CORES = 2
TOK = 128
BLK = 128

beta_one = 0.9
beta_two = 0.95
adam_eps = 1e-08
learn_rate = 0.02
decay_rate = 0.1
lasso_weight = 2.0
norm_eps = 1e-06

MESH = pl.DeviceIdType.MESH
F32 = jnp.float32
BF16 = jnp.bfloat16
NT = (((1,), (1,)), ((), ()))


def kernel(
    nz, acts, p_tail, m1_tail, m2_tail, fixes, p_hbm, m1_hbm, m2_hbm,
    gh_out, ga_out, up_out, n1_out, n2_out, factor_out,
    p1, m1, m2, p2, o1, o2, pw, gb, gw,
    lb, rg, lt, ll, lown,
    wins, rbuf, pb, xs, xr, ring, yb, bias_own, bias_grp, bias_got,
    ext_ref, acc_ref, s_own, s_grp,
    in_sem, out_sem, self_sem, s_ry, r_ry, s_lf, r_lf, s_lx, r_lx,
    s_bg, r_bg, s_by, r_by, s_rz, r_rz, s_r1, r_r1, s_r2, r_r2, s_rp, r_rp,
    s_sp, r_sp, s_sr, r_sr, s_sy, r_sy, s_sg, r_sg,
):
    h_in, gq_in, a_in, go_in = (acts.at[i] for i in range(4))
    nf = NY * nz * CORES
    nb = NY * nz
    dim = nb * BLK
    half_y = NY // 2
    longs, shorts = nz // 2, nz - 1 - nz // 2
    x = lax.axis_index("dp")
    f = lax.axis_index("fsdp")
    c = f % CORES
    z = (f // CORES) % nz
    y = f // (CORES * nz)
    h = y // half_y
    m = f // 2
    par = f % 2
    k = f // CORES
    sig = 1 - 2 * c

    def fid(yy, zz, cc):
        return (yy * nz + zz) * CORES + cc

    def zw(v):
        return (v + 2 * nz) % nz

    partner = fid(y, z, 1 - c)
    z_long = fid(y, zw(z + sig), c)
    z_short = fid(y, zw(z - sig), c)
    x_up = (x + 1) % NX
    x_down = (x + NX - 1) % NX
    x_far = (x + 2) % NX

    pending = []

    def send(src, dst, ss, rs, xx, ff):
        copy = pltpu.make_async_remote_copy(
            src_ref=src, dst_ref=dst, send_sem=ss, recv_sem=rs,
            device_id=(xx, ff), device_id_type=MESH,
        )
        copy.start()
        return copy

    def send_later(*args):
        pending.append(send(*args))

    def arrive(dst, rs):
        pltpu.make_async_remote_copy(
            src_ref=dst, dst_ref=dst, send_sem=s_by, recv_sem=rs,
            device_id=(x, partner), device_id_type=MESH,
        ).wait_recv()

    cells = nb * BLK * BLK
    loads = [
        pltpu.make_async_copy(src.at[pl.ds(0, cells)], dst, in_sem.at[i])
        for i, (src, dst) in enumerate(((p_hbm, p1), (m1_hbm, m1), (m2_hbm, m2)))
    ]
    for load in loads:
        load.start()

    barrier = pltpu.get_barrier_semaphore()

    def greet(xx, ff):
        pl.semaphore_signal(barrier, inc=1, device_id=(xx, ff), device_id_type=MESH)

    group = [(dz, dc) for dz in range(nz) for dc in range(CORES) if (dz, dc) != (0, 0)]
    for dz, dc in group:
        greet(x, fid(y, zw(z + dz), (c + dc) % CORES))
    for dy in range(1, NY):
        for dc in range(CORES):
            greet(x, fid((y + dy) % NY, z, (c + dc) % CORES))
    for dx in range(1, NX):
        greet((x + dx) % NX, f)
    fl = f % (nf // 2)
    row_src = 2 * (fl + 1 - 2 * h) + h
    row_chip = fl + 1 - 2 * h
    has_row = (row_chip >= 0) & (row_chip < nf // 2)
    left_dsts = (k, nf // 2 + k)
    left_srcs = (2 * fl, 2 * fl + 1)
    row_dst_low = k - 1 + 2 * c
    gives_row = (row_dst_low >= 0) & (row_dst_low < nf // 2)
    row_dst = c * (nf // 2) + row_dst_low

    for src in left_srcs:

        @pl.when(src != f)
        def _(src=src):
            greet(x, src)

    @pl.when(has_row)
    def _():
        greet(x, row_src)

    greeted = len(group) + (NY - 1) * CORES + NX - 1
    for dst in left_dsts:
        greeted = greeted + (dst != f).astype(jnp.int32)
    greeted = greeted + gives_row.astype(jnp.int32)
    lane = lax.broadcasted_iota(jnp.int32, (BLK, BLK), 1)
    row = lax.broadcasted_iota(jnp.int32, (BLK, BLK), 0)
    low = lane < 64

    pl.semaphore_wait(barrier, greeted)

    own_half = pl.ds(pl.multiple_of(c * 64, 64), 64)

    def right_sends():
        for yd in range(NY):
            src = h_in if yd < half_y else a_in
            for cc in range(CORES):
                yield yd, cc, src

    for yd, cc, src in right_sends():
        remote = (yd != y) | (cc != c)

        @pl.when(remote)
        def _(yd=yd, cc=cc, src=src):
            send(
                src, rbuf.at[x, z, y, own_half], s_ry.at[yd, cc], r_ry.at[y, c], x, fid(yd, z, cc)
            )

        @pl.when(jnp.logical_not(remote))
        def _(src=src):
            pltpu.make_async_copy(src, rbuf.at[x, z, y, own_half], self_sem.at[0]).start()

    row_part = lambda src: src.at[pl.ds(pl.multiple_of(c * (64 - 16), 16), 16)]
    for i, (src, dst) in enumerate(zip((gq_in, go_in), left_dsts)):

        @pl.when(dst != f)
        def _(i=i, src=src, dst=dst):
            send(src, lb.at[x, own_half], s_lf.at[i], r_lf.at[c], x, dst)

        @pl.when(dst == f)
        def _(src=src):
            pltpu.make_async_copy(src, lb.at[x, own_half], self_sem.at[1]).start()

        @pl.when(gives_row & (c == i))
        def _(src=src):
            send(row_part(src), rg.at[x], s_lf.at[2], r_lf.at[2], x, row_dst)

    @pl.when(jnp.logical_not(has_row))
    def _():
        rg[x] = jnp.zeros((16, TOK), BF16)

    loads[0].wait()
    group_cells = 8 * dim

    @pl.loop(0, BLK // 8)
    def _(i):
        some = p1[pl.ds(i * group_cells, group_cells)].reshape(8, nb, BLK)
        pw[:, pl.ds(pl.multiple_of(i * 8, 8), 8), :] = jnp.swapaxes(some, 0, 1)

    pair = lambda cc: pl.ds(half_y * cc, half_y)
    def own_quad():
        for yy in range(NY):
            for cc in range(CORES):
                remote = (yy != y) | (cc != c)
                half = rbuf.at[x, z, yy, pl.ds(cc * 64, 64)]

                @pl.when(remote)
                def _(yy=yy, cc=cc, half=half):
                    arrive(half, r_ry.at[yy, cc])

        pltpu.make_async_copy(h_in, rbuf.at[x, z, y, own_half], self_sem.at[0]).wait()

    def z_quad(r):
        out = []
        if r == 0:
            return [(0, z)]
        if r <= longs:
            out.append((2 * r - 1, zw(z - sig * r)))
        if r <= shorts:
            out.append((2 * r, zw(z + sig * r)))
        return out

    def round_a(r):
        for idx, zq in z_quad(r):
            ref = rbuf.at[x, zq, pair(c)]
            if r > 0:
                arrive(ref, r_rz.at[idx])
            is_long = r == 0 or idx % 2 == 1
            is_short = r == 0 or idx % 2 == 0
            if is_long and r < longs:
                send_later(ref, ref, s_rz.at[2 * r + 1], r_rz.at[2 * r + 1], x, z_long)
            if is_short and r < shorts:
                send_later(ref, ref, s_rz.at[2 * r + 2], r_rz.at[2 * r + 2], x, z_short)
            send_later(ref, ref, s_r1.at[idx, 0], r_r1.at[idx, 0], x_up, f)
            send_later(ref, ref, s_r1.at[idx, 1], r_r1.at[idx, 1], x_down, f)
            if r > 0:
                send_later(ref, ref, s_rp.at[x, zq], r_rp.at[x, zq], x, partner)

    def round_x1(r):
        for idx, zq in z_quad(r):
            for way, (frm, to) in enumerate(((x_down, x_up), (x_up, x_down))):
                ref = rbuf.at[frm, zq, pair(c)]
                arrive(ref, r_r1.at[idx, way])
                part = rbuf.at[frm, zq, half_y * c + way]
                send_later(part, part, s_r2.at[idx, way], r_r2.at[idx, way], to, f)
                send_later(ref, ref, s_rp.at[frm, zq], r_rp.at[frm, zq], x, partner)

    def round_x2(r):
        for idx, zq in z_quad(r):
            for way in range(2):
                arrive(rbuf.at[x_far, zq, half_y * c + way], r_r2.at[idx, way])
            ref = rbuf.at[x_far, zq, pair(c)]
            send_later(ref, ref, s_rp.at[x_far, zq], r_rp.at[x_far, zq], x, partner)

    own_quad()
    round_a(0)

    lane_row = lax.broadcasted_iota(jnp.int32, (1, BLK), 1)

    def tail_row(ref):
        return jnp.where(lane_row < 64, ref[...].reshape(8, BLK)[0:1], 0.0)

    tail_p = tail_row(p_tail)
    tail_here = jnp.where(
        par == 1, pltpu.roll(jnp.broadcast_to(tail_p, (8, BLK)), 64, 1)[0:1], tail_p
    )

    def window_block(j):
        first = pw[(j - m + nb) % nb]
        second = pw[(j - m - 1 + nb) % nb]
        mixed = pltpu.roll(jnp.where(low, first, second), 64, 1)
        block = jnp.where(par == 1, mixed, first)
        column = j * BLK + lane
        carried = column < 64 * f
        top = jnp.where(carried, 0.0, block)
        bottom = jnp.where(carried, block, 0.0)
        is_tail = (row == BLK - 1) & (column >= 64 * f) & (column < 64 * f + 64)
        bottom = jnp.where(is_tail, tail_here, bottom)
        return jnp.concatenate([top, bottom], axis=0).astype(BF16)

    @pl.loop(0, nz)
    def _(d):
        for hh in range(2):
            for i in range(half_y):
                wins[d, hh, :, i * BLK : (i + 1) * BLK] = window_block((half_y * hh + i) * nz + d)

    for cc, src in enumerate(left_srcs):

        @pl.when(src != f)
        def _(cc=cc):
            arrive(lb.at[x, pl.ds(cc * 64, 64)], r_lf.at[cc])

        @pl.when(src == f)
        def _():
            pltpu.make_async_copy(gq_in, lb.at[x, own_half], self_sem.at[1]).wait()

    @pl.when(has_row)
    def _():
        arrive(rg.at[x], r_lf.at[2])

    for dx in range(1, NX):
        xx = (x + dx) % NX
        send_later(lb.at[x], lb.at[x], s_lx.at[dx - 1, 0], r_lx.at[x, 0], xx, f)
        send_later(rg.at[x], rg.at[x], s_lx.at[dx - 1, 1], r_lx.at[x, 1], xx, f)

    def build_left(xx):
        lt[pl.ds(0, 16), :] = rg[xx].astype(F32)
        lt[pl.ds(16, BLK), :] = lb[xx].astype(F32)
        lt[pl.ds(16 + BLK, 16), :] = rg[xx].astype(F32)
        before = lt[pl.ds(15, BLK), :]
        middle = lt[pl.ds(16, BLK), :]
        after = lt[pl.ds(17, BLK), :]
        zero = jnp.where(h == 0, middle, before)
        one = jnp.where(h == 0, after, middle)
        return zero, one

    zero, one = build_left(x)
    lown[:, pl.ds(0, BLK)] = jnp.transpose(zero).astype(BF16)
    lown[:, pl.ds(BLK, BLK)] = jnp.transpose(one).astype(BF16)

    def partial_chunk(d):
        for mine in range(2):
            hh = c if mine == 0 else 1 - c
            part = jnp.dot(lown[...], wins[d, hh], preferred_element_type=F32)
            for i in range(half_y):
                target = pb if mine == 0 else xs
                target[d, i] = part[:, i * BLK : (i + 1) * BLK]
        send_later(xs.at[d], xr.at[d], s_sp.at[d], r_sp.at[d], x, partner)

    def round_c(r):
        if r >= longs:
            return
        partial_chunk(zw(z + sig * (longs - r)))
        partial_chunk(zw(z - sig * (shorts - r)))

    def chip_sum(d):
        arrive(xr.at[d], r_sp.at[d])
        return pb[d] + xr[d]

    def round_e(r):
        for way, (hops, to, sign) in enumerate(((longs, z_long, 1), (shorts, z_short, -1))):
            if r >= hops:
                continue
            d = zw(z + sig * sign * (hops - r))
            slot = 2 * r + way
            if r == 0:
                pb[d] = chip_sum(d)
                src = pb.at[d]
            else:
                before = slot - 2
                arrive(ring.at[before], r_sr.at[before])
                ring[before] = ring[before] + chip_sum(d)
                src = ring.at[before]
            send_later(src, ring.at[slot], s_sr.at[slot], r_sr.at[slot], x, to)

    def finish_sums():
        total = chip_sum(z)
        slot = 2 * (longs - 1)
        arrive(ring.at[slot], r_sr.at[slot])
        total = total + ring[slot]
        if shorts:
            slot = 2 * (shorts - 1) + 1
            arrive(ring.at[slot], r_sr.at[slot])
            total = total + ring[slot]
        pb[z] = total
        for i in range(half_y):
            for cc in range(CORES):
                yd = half_y * c + i

                @pl.when((yd != y) | (cc != c))
                def _(i=i, cc=cc, yd=yd):
                    send(pb.at[z, i], yb.at[y], s_sy.at[i, cc], r_sy.at[y], x, fid(yd, z, cc))

        @pl.when(h == c)
        def _():
            yb[y] = pb[z, y % half_y]

    def write_cotangents():
        for yy in range(NY):

            @pl.when((yy != y) | (h != c))
            def _(yy=yy):
                arrive(yb.at[yy], r_sy.at[yy])

        for out, base_y in ((gh_out, 0), (ga_out, half_y)):
            total = yb[base_y]
            for i in range(1, half_y):
                total = total + yb[base_y + i]
            total = jnp.transpose(total)
            out[...] = jnp.where(c == 1, total[64:], total[:64]).astype(BF16)

    def full_left():
        for xx in range(NX):

            @pl.when(xx != x)
            def _(xx=xx):
                arrive(lb.at[xx], r_lx.at[xx, 0])
                arrive(rg.at[xx], r_lx.at[xx, 1])

            zero, one = build_left(xx)
            ll[pl.ds(0, BLK), pl.ds(xx * TOK, TOK)] = zero.astype(BF16)
            ll[pl.ds(BLK, BLK), pl.ds(xx * TOK, TOK)] = one.astype(BF16)
        bias_own[...] = lax.dot_general(
            jnp.ones((8, NX * TOK), BF16), ll[pl.ds(0, BLK), :], NT, preferred_element_type=F32
        )
        me = z * CORES + c
        bias_grp[pl.ds(pl.multiple_of(me * 8, 8), 8), :] = bias_own[...]
        for i, (dz, dc) in enumerate(group):
            zz, cc = zw(z + dz), (c + dc) % CORES
            mine = bias_grp.at[pl.ds(pl.multiple_of(me * 8, 8), 8)]
            send_later(bias_own, mine, s_bg.at[i], r_bg.at[me], x, fid(y, zz, cc))

    def bias_on():
        for dz, dc in group:
            other = zw(z + dz) * CORES + (c + dc) % CORES
            arrive(bias_grp.at[pl.ds(pl.multiple_of(other * 8, 8), 8)], r_bg.at[other])
        send_later(bias_grp, bias_got, s_by, r_by, x, fid((y + 1) % NY, z, c))

    ext_ref[...] = jnp.zeros((8, BLK), F32)

    def gradient_quad(r):
        for _, zq in z_quad(r):
            for xx in range(NX):
                if r == 0:

                    @pl.when(xx != x)
                    def _(xx=xx, zq=zq):
                        arrive(rbuf.at[xx, zq, pair(1 - c)], r_rp.at[xx, zq])
                else:
                    arrive(rbuf.at[xx, zq, pair(1 - c)], r_rp.at[xx, zq])
            for yy in range(0, NY, 2):
                wide = jnp.concatenate(
                    [
                        jnp.concatenate([rbuf[xx, zq, yy], rbuf[xx, zq, yy + 1]], axis=0)
                        for xx in range(NX)
                    ],
                    axis=1,
                )
                both = lax.dot_general(ll[...], wide, NT, preferred_element_type=F32)
                for i in range(2):
                    j = (yy + i) * nz + zq
                    p_zero = both[:BLK, i * BLK : (i + 1) * BLK]
                    p_one = both[BLK:, i * BLK : (i + 1) * BLK]
                    carried = j * BLK + lane < 64 * f
                    gw[j] = jnp.where(carried, p_one, p_zero)
                    ext_ref[...] = ext_ref[...] + jnp.where(
                        j == m, p_one[BLK - 8 :, :], jnp.zeros((8, BLK), F32)
                    )

    def reorder(zc):
        for yy in range(NY):
            j = yy * nz + zc
            first = gw[j]
            second = gw[(j + 1) % nb]
            mixed = pltpu.roll(jnp.where(low, second, first), 64, 1)
            gb[(j - m + nb) % nb] = jnp.where(par == 1, mixed, first)

    def gradient(r):
        gradient_quad(r)
        if 0 < r <= longs:
            reorder(zw(z - r))
            reorder(zw(z + r - 1))

    def bias_rows():
        arrive(bias_got, r_by)
        half = nb // 2
        sums = bias_got[pl.ds(0, half, stride=8), :]
        turned = pltpu.roll(sums, 64, 1)
        index = lax.broadcasted_iota(jnp.int32, (half, BLK), 0)
        before = jnp.where(index == 0, 0.0, pltpu.roll(turned, 1, 0))
        left_half = lax.broadcasted_iota(jnp.int32, (half, BLK), 1) < 64
        nothing = jnp.zeros((half, BLK), F32)
        last = jnp.where(left_half, before, turned)
        here_first = f == nf // 2
        here_last = f == nf // 2 - 1
        ext_ref[...] = ext_ref[...] + jnp.where(here_last, sums[half - 1 : half], 0.0)
        return (
            jnp.where(here_first, jnp.concatenate([sums, nothing], axis=0), 0.0),
            jnp.where(here_last, jnp.concatenate([nothing, last], axis=0), 0.0),
        )

    round_c(0)
    round_c(1)
    round_a(1)
    round_e(0)
    round_x1(0)
    round_c(2)
    round_a(2)
    round_x1(1)
    round_x2(0)
    round_c(3)
    full_left()
    round_a(3)
    round_e(1)
    round_x1(2)
    round_x2(1)
    gradient(0)
    round_a(4)
    round_e(2)
    round_x1(3)
    round_x2(2)
    bias_on()
    gradient(1)
    round_x1(4)
    round_x2(3)
    round_e(3)
    gradient(2)
    round_x2(4)
    gradient(3)
    gradient(4)
    bias_first, bias_last = bias_rows()

    one_scale = 1.0 / fixes[0]
    two_scale = 1.0 / fixes[1]

    def adam(grad, param, mom_one, mom_two):
        new_one = beta_one * mom_one + (1.0 - beta_one) * grad
        new_two = beta_two * mom_two + (1.0 - beta_two) * grad * grad
        direction = (new_one * one_scale) / (jnp.sqrt(new_two * two_scale) + adam_eps)
        return new_one, new_two, param - learn_rate * (direction + decay_rate * param)

    loads[1].wait()
    loads[2].wait()
    rows_each = 8
    span = rows_each * nb
    steps = BLK // rows_each

    def adam_rows(i, bias_top=None, bias_bottom=None):
        at = pl.ds(pl.multiple_of(i * span, span), span)
        flat = pl.ds(pl.multiple_of(i * span * BLK, span * BLK), span * BLK)
        grad = gb[:, pl.ds(pl.multiple_of(i * rows_each, rows_each), rows_each), :]
        grad = jnp.swapaxes(grad, 0, 1)
        if bias_top is not None:
            grad = jnp.concatenate([grad[:1] + bias_top[None], grad[1:]], axis=0)
        if bias_bottom is not None:
            grad = jnp.concatenate([grad[:-1], grad[-1:] + bias_bottom[None]], axis=0)
        new_one, new_two, updated = adam(
            grad.reshape(span, BLK),
            p1[flat].reshape(span, BLK),
            m1[flat].reshape(span, BLK),
            m2[flat].reshape(span, BLK),
        )
        o1[at, :] = new_one
        o2[at, :] = new_two
        p2[at, :] = updated
        return (updated * updated).reshape(rows_each, nb, BLK)

    acc_ref[...] = jnp.sum(adam_rows(0, bias_top=bias_first), axis=0)

    @pl.loop(1, steps - 1)
    def _(i):
        acc_ref[...] = acc_ref[...] + jnp.sum(adam_rows(i), axis=0)

    squares = adam_rows(steps - 1, bias_bottom=bias_last)
    acc_main = acc_ref[...] + jnp.sum(squares[: rows_each - 1], axis=0)
    acc_last = squares[rows_each - 1]
    ext_row = ext_ref[...]
    ext_row = jnp.where(par == 1, pltpu.roll(ext_row, 64, 1), ext_row)[7:8]
    ext_one, ext_two, ext_up = adam(
        ext_row, tail_p, tail_row(m1_tail), tail_row(m2_tail)
    )
    o1[pl.ds(nb * BLK, 8), :] = jnp.broadcast_to(ext_one, (8, BLK))
    o2[pl.ds(nb * BLK, 8), :] = jnp.broadcast_to(ext_two, (8, BLK))
    p2[pl.ds(nb * BLK, 8), :] = jnp.broadcast_to(ext_up, (8, BLK))
    writes = [
        pltpu.make_async_copy(p2, up_out, out_sem.at[2]),
        pltpu.make_async_copy(o1, n1_out, out_sem.at[0]),
        pltpu.make_async_copy(o2, n2_out, out_sem.at[1]),
    ]
    for write in writes:
        write.start()

    heads = lax.broadcasted_iota(jnp.int32, (nb, BLK), 1)
    blocks = lax.broadcasted_iota(jnp.int32, (nb, BLK), 0)
    low_b = heads < 64
    ext_sq = jnp.sum(jnp.where(lane_row < 64, ext_up * ext_up, 0.0), axis=1, keepdims=True)

    def head_of(part):
        spot = f + 2 * blocks + part
        carry = spot // nf
        by_column = (spot % nf) // 2
        main = jnp.where(h == 0, f, by_column)
        last_q = jnp.where(f + carry < nf // 2, f + carry, by_column)
        return main, last_q

    ext_head = jnp.where(f + 1 < nf // 2, f + 1, f // 2)
    total = jnp.where(lane_row == ext_head, ext_sq, 0.0)
    maps = [head_of(0), head_of(1)]
    for part in range(2):
        inside = low_b if part == 0 else jnp.logical_not(low_b)
        for which, acc in enumerate((acc_main, acc_last)):
            sums = jnp.sum(jnp.where(inside, acc, 0.0), axis=1, keepdims=True)
            total = total + jnp.sum(
                jnp.where(maps[part][which] == heads, sums, 0.0), axis=0, keepdims=True
            )
    s_own[...] = total
    offsets = [
        (dy, dz, dc)
        for dy in range(NY)
        for dz in range(nz)
        for dc in range(CORES)
        if (dy, dz, dc) != (0, 0, 0)
    ]
    offsets.sort(key=lambda o: -(min(o[0], NY - o[0]) + min(o[1], nz - o[1])))
    for i, (dy, dz, dc) in enumerate(offsets):
        target = fid((y + dy) % NY, zw(z + dz), (c + dc) % CORES)
        send(s_own, s_grp.at[i], s_sg, r_sg, x, target)
    finish_sums()
    arrive(s_grp, r_sg)
    sumsq = s_own[...] + jnp.sum(s_grp[...], axis=0)
    threshold = learn_rate * lasso_weight * math.sqrt(2 * HD * dim + HD)
    shrink = jnp.maximum(1.0 - threshold / jnp.sqrt(sumsq + norm_eps), 0.0)

    def factor(which):
        sides = [
            jnp.sum(jnp.where(maps[part][which] == heads, shrink, 0.0), axis=1, keepdims=True)
            for part in range(2)
        ]
        return jnp.where(low_b, sides[0], sides[1])

    factor_out[pl.ds(0, nb), :] = factor(0)
    factor_out[pl.ds(nb, nb), :] = factor(1)
    ext_shrink = jnp.sum(jnp.where(lane_row == ext_head, shrink, 0.0), axis=1, keepdims=True)
    factor_out[pl.ds(2 * nb, 8), :] = jnp.broadcast_to(ext_shrink, (8, BLK))

    write_cotangents()

    def sent(src, ss):
        pltpu.make_async_remote_copy(
            src_ref=src, dst_ref=src, send_sem=ss, recv_sem=r_by,
            device_id=(x, partner), device_id_type=MESH,
        ).wait_send()

    sent(s_grp, s_sg)
    for copy in pending:
        copy.wait_send()
    for yd, cc, src in right_sends():

        @pl.when((yd != y) | (cc != c))
        def _(yd=yd, cc=cc, src=src):
            sent(src, s_ry.at[yd, cc])

    for i in range(half_y):
        for cc in range(CORES):
            yd = half_y * c + i

            @pl.when((yd != y) | (cc != c))
            def _(i=i, cc=cc):
                sent(pb.at[z, i], s_sy.at[i, cc])

    for i, (src, dst) in enumerate(zip((gq_in, go_in), left_dsts)):

        @pl.when(dst != f)
        def _(i=i, src=src):
            sent(src, s_lf.at[i])

    @pl.when(gives_row)
    def _():
        sent(row_part(gq_in), s_lf.at[2])

    for write in writes:
        write.wait()


def finish(nb, gh, ga, up, n1, n2, factors, gh_out, ga_out, np_out, n1_out, n2_out, scaled, sems):
    copies = [
        pltpu.make_async_copy(gh, gh_out, sems.at[6]),
        pltpu.make_async_copy(ga, ga_out, sems.at[7]),
        pltpu.make_async_copy(n1, n1_out, sems.at[0]),
        pltpu.make_async_copy(n2, n2_out, sems.at[1]),
    ]
    for copy in copies:
        copy.start()
    pieces, rows_each = 4, 4
    span = rows_each * nb
    steps = BLK // rows_each // pieces
    main = factors[pl.ds(0, nb), :]
    for piece in range(pieces):
        start = piece * steps * span
        full = steps - 1 if piece == pieces - 1 else steps

        @pl.loop(0, full)
        def _(i):
            at = pl.ds(pl.multiple_of(start + i * span, span), span)
            block = up[at, :].reshape(rows_each, nb, BLK) * factors[pl.ds(0, nb), :][None]
            scaled[at, :] = block.reshape(span, BLK)

        rows = steps * span
        if piece == pieces - 1:
            at = pl.ds(start + full * span, span - nb)
            block = up[at, :].reshape(rows_each - 1, nb, BLK) * main[None]
            scaled[at, :] = block.reshape(span - nb, BLK)
            at = pl.ds(nb * BLK - nb, nb)
            scaled[at, :] = up[at, :] * factors[pl.ds(nb, nb), :]
            at = pl.ds(nb * BLK, 8)
            scaled[at, :] = up[at, :] * factors[pl.ds(2 * nb, 8), :]
            rows += 8
        at = pl.ds(start, rows)
        copy = pltpu.make_async_copy(scaled.at[at], np_out.at[at], sems.at[2 + piece])
        copy.start()
        copies.append(copy)
    for copy in copies:
        copy.wait()


def on_device(
    nz, hidden, grad_query, attn_out, grad_output, flat_params, moment_one, moment_two, step_count
):
    nb = NY * nz
    cells = nb * BLK * BLK
    rows = nb * BLK
    shard_len = flat_params.shape[0]
    step_num = step_count[0].astype(F32)
    fixes = jnp.stack(
        [
            1.0 - jnp.power(jnp.float32(beta_one), step_num),
            1.0 - jnp.power(jnp.float32(beta_two), step_num),
        ]
    )
    vm = lambda shape, dtype=F32: pltpu.VMEM(shape, dtype)
    dma = lambda *shape: pltpu.SemaphoreType.DMA(shape) if shape else pltpu.SemaphoreType.DMA
    grp = nz * CORES
    whole = pl.BlockSpec(memory_space=pltpu.VMEM)
    anywhere = pl.BlockSpec(memory_space=pl.ANY)
    scratch = [
        vm((cells,)), vm((cells,)), vm((cells,)),
        vm((rows + 8, BLK)), vm((rows + 8, BLK)), vm((rows + 8, BLK)),
        vm((nb, BLK, BLK)), vm((nb, BLK, BLK)), vm((nb, BLK, BLK)),
        vm((NX, BLK, TOK), BF16), vm((NX, 16, TOK), BF16),
        vm((BLK + 32, TOK)), vm((2 * BLK, NX * TOK), BF16), vm((TOK, 2 * BLK), BF16),
        vm((nz, 2, 2 * BLK, NY // 2 * BLK), BF16), vm((NX, nz, NY, TOK, BLK), BF16),
        vm((nz, NY // 2, TOK, BLK)), vm((nz, NY // 2, TOK, BLK)), vm((nz, NY // 2, TOK, BLK)),
        vm((nz, NY // 2, TOK, BLK)), vm((NY, TOK, BLK)),
        vm((8, BLK)), vm((grp * 8, BLK)), vm((grp * 8, BLK)),
        vm((8, BLK)), vm((nb, BLK)),
        vm((1, BLK)), vm((NY * grp - 1, 1, BLK)),
        dma(3), dma(3), dma(2), dma(NY, CORES), dma(NY, CORES), dma(3), dma(3),
        dma(NX - 1, 2), dma(NX, 2),
        dma(grp - 1), dma(grp), dma(), dma(), dma(nz), dma(nz), dma(nz, 2), dma(nz, 2),
        dma(nz, 2), dma(nz, 2), dma(NX, nz), dma(NX, nz),
        dma(nz), dma(nz), dma(nz), dma(nz), dma(NY // 2, CORES), dma(NY),
        dma(), dma(),
    ]
    cotangent = jax.ShapeDtypeStruct((64, TOK), BF16)
    flat = jax.ShapeDtypeStruct((rows + 8, BLK), F32)
    tail = pl.BlockSpec((1024,), lambda i: (cells // 1024,))
    outs = pl.pallas_call(
        functools.partial(kernel, nz),
        grid=(1,),
        out_shape=[
            cotangent, cotangent,
            flat, flat, flat,
            jax.ShapeDtypeStruct((2 * nb + 8, BLK), F32),
        ],
        in_specs=[anywhere] + [tail] * 3 + [pl.BlockSpec(memory_space=pltpu.SMEM)] + [anywhere] * 3,
        out_specs=[whole] * 2 + [anywhere] * 3 + [whole],
        scratch_shapes=scratch,
        compiler_params=pltpu.CompilerParams(
            collective_id=0, has_side_effects=True, vmem_limit_bytes=46 * 1024 * 1024
        ),
        cost_estimate=pl.CostEstimate(
            flops=4 * 512 * 128 * 4096, bytes_accessed=6 * 2 * 1024 * 1024, transcendentals=524352
        ),
        name="step",
    )(
        jnp.stack([hidden.T, grad_query.T, attn_out.T, grad_output.T]),
        flat_params, moment_one, moment_two, fixes, flat_params, moment_one, moment_two,
    )
    results = pl.pallas_call(
        functools.partial(finish, nb),
        out_shape=[cotangent] * 2 + [flat] * 3,
        in_specs=[anywhere, anywhere, whole, anywhere, anywhere, whole],
        out_specs=[anywhere] * 5,
        scratch_shapes=[vm((rows + 8, BLK)), dma(8)],
        compiler_params=pltpu.CompilerParams(vmem_limit_bytes=16 * 1024 * 1024),
        name="finish",
    )(*outs)
    grad_hidden, grad_attn = results[0].T, results[1].T
    new_params, new_one, new_two = (part.reshape(-1)[:shard_len] for part in results[2:])
    return (grad_hidden, grad_attn, new_params, new_one, new_two)


def solution(mesh):
    nz = mesh.shape["fsdp"] // (NY * CORES)
    in_specs = (
        P("dp", "fsdp"),
        P("dp", "fsdp"),
        P("dp", "fsdp"),
        P("dp", "fsdp"),
        P("fsdp"),
        P("fsdp"),
        P("fsdp"),
        P(),
    )
    out_specs = (P("dp", "fsdp"), P("dp", "fsdp"), P("fsdp"), P("fsdp"), P("fsdp"))
    return jax.shard_map(
        functools.partial(on_device, nz), mesh=mesh, in_specs=in_specs, out_specs=out_specs, check_vma=False
    )
```

```python
import functools
import math

import jax
import jax.numpy as jnp
from jax import lax
from jax.experimental import pallas as pl
from jax.experimental.pallas import tpu as pltpu
from jax.sharding import PartitionSpec as P

HD = 128
NX = 4
NY = 4
CORES = 2
TOK = 128
BLK = 128
DIRECT = 4

beta_one = 0.9
beta_two = 0.95
adam_eps = 1e-08
learn_rate = 0.02
decay_rate = 0.1
lasso_weight = 2.0
norm_eps = 1e-06

MESH = pl.DeviceIdType.MESH
F32 = jnp.float32
BF16 = jnp.bfloat16
NT = (((1,), (1,)), ((), ()))


def kernel(
    nz, acts, p_tail, m1_tail, m2_tail, fixes, p_hbm, m1_hbm, m2_hbm,
    gh_out, ga_out, up_out, n1_out, n2_out, factor_out,
    p1, m1, m2, p2, o1, o2, pw, gb, gw,
    lb, rg, lt, ll, lown,
    wins, rbuf, pb, xs, xr, ring, yb, bias_own, bias_got, bias_add,
    ext_ref, acc_ref, s_own, s_grp,
    in_sem, out_sem, self_sem, s_ry, r_ry, s_lf, r_lf, s_lx, r_lx,
    s_by, r_by, s_rz, r_rz, s_r1, r_r1, s_r2, r_r2, s_rp, r_rp,
    s_sp, r_sp, s_sr, r_sr, s_sy, r_sy, s_sg, r_sg,
):
    h_in, gq_in, a_in, go_in = (acts.at[i] for i in range(4))
    nf = NY * nz * CORES
    nb = NY * nz
    dim = nb * BLK
    half_y = NY // 2
    longs, shorts = nz // 2, nz - 1 - nz // 2
    x = lax.axis_index("dp")
    f = lax.axis_index("fsdp")
    c = f % CORES
    z = (f // CORES) % nz
    y = f // (CORES * nz)
    h = y // half_y
    m = f // 2
    par = f % 2
    k = f // CORES
    sig = 1 - 2 * c

    def fid(yy, zz, cc):
        return (yy * nz + zz) * CORES + cc

    def zw(v):
        return (v + 2 * nz) % nz

    partner = fid(y, z, 1 - c)
    z_long = fid(y, zw(z + sig), c)
    z_short = fid(y, zw(z - sig), c)
    x_up = (x + 1) % NX
    x_down = (x + NX - 1) % NX
    x_far = (x + 2) % NX

    pending = []

    def send(src, dst, ss, rs, xx, ff):
        copy = pltpu.make_async_remote_copy(
            src_ref=src, dst_ref=dst, send_sem=ss, recv_sem=rs,
            device_id=(xx, ff), device_id_type=MESH,
        )
        copy.start()
        return copy

    def send_later(*args):
        pending.append(send(*args))

    def arrive(dst, rs):
        pltpu.make_async_remote_copy(
            src_ref=dst, dst_ref=dst, send_sem=s_by, recv_sem=rs,
            device_id=(x, partner), device_id_type=MESH,
        ).wait_recv()

    cells = nb * BLK * BLK
    loads = [
        pltpu.make_async_copy(src.at[pl.ds(0, cells)], dst, in_sem.at[i])
        for i, (src, dst) in enumerate(((p_hbm, p1), (m1_hbm, m1), (m2_hbm, m2)))
    ]

    barrier = pltpu.get_barrier_semaphore()

    def greet(xx, ff):
        pl.semaphore_signal(barrier, inc=1, device_id=(xx, ff), device_id_type=MESH)

    near_z = sorted({1, nz - 1})
    for dz in near_z:
        greet(x, fid(y, zw(z + dz), c))
    greet(x, partner)
    for dy in range(1, NY):
        for dc in range(CORES):
            greet(x, fid((y + dy) % NY, z, (c + dc) % CORES))
    for dx in range(1, NX):
        greet((x + dx) % NX, f)
    fl = f % (nf // 2)
    row_src = 2 * (fl + 1 - 2 * h) + h
    row_chip = fl + 1 - 2 * h
    has_row = (row_chip >= 0) & (row_chip < nf // 2)
    left_dsts = (k, nf // 2 + k)
    left_srcs = (2 * fl, 2 * fl + 1)
    row_dst_low = k - 1 + 2 * c
    gives_row = (row_dst_low >= 0) & (row_dst_low < nf // 2)
    row_dst = c * (nf // 2) + row_dst_low

    for src in left_srcs:

        @pl.when(src != f)
        def _(src=src):
            greet(x, src)

    @pl.when(has_row)
    def _():
        greet(x, row_src)

    greeted = len(near_z) + 1 + (NY - 1) * CORES + NX - 1
    for dst in left_dsts:
        greeted = greeted + (dst != f).astype(jnp.int32)
    greeted = greeted + gives_row.astype(jnp.int32)
    lane = lax.broadcasted_iota(jnp.int32, (BLK, BLK), 1)
    row = lax.broadcasted_iota(jnp.int32, (BLK, BLK), 0)
    low = lane < 64

    pl.semaphore_wait(barrier, greeted)

    own_half = pl.ds(pl.multiple_of(c * 64, 64), 64)

    def right_sends():
        for yd in range(NY):
            src = h_in if yd < half_y else a_in
            for cc in range(CORES):
                yield yd, cc, src

    for yd, cc, src in right_sends():
        remote = (yd != y) | (cc != c)

        @pl.when(remote)
        def _(yd=yd, cc=cc, src=src):
            send(
                src, rbuf.at[x, z, y, own_half], s_ry.at[yd, cc], r_ry.at[y, c], x, fid(yd, z, cc)
            )

        @pl.when(jnp.logical_not(remote))
        def _(src=src):
            pltpu.make_async_copy(src, rbuf.at[x, z, y, own_half], self_sem.at[0]).start()

    row_part = lambda src: src.at[pl.ds(pl.multiple_of(c * (64 - 16), 16), 16)]
    for i, (src, dst) in enumerate(zip((gq_in, go_in), left_dsts)):

        @pl.when(dst != f)
        def _(i=i, src=src, dst=dst):
            send(src, lb.at[x, own_half], s_lf.at[i], r_lf.at[c], x, dst)

        @pl.when(dst == f)
        def _(src=src):
            pltpu.make_async_copy(src, lb.at[x, own_half], self_sem.at[1]).start()

        @pl.when(gives_row & (c == i))
        def _(src=src):
            send(row_part(src), rg.at[x], s_lf.at[2], r_lf.at[2], x, row_dst)

    @pl.when(jnp.logical_not(has_row))
    def _():
        rg[x] = jnp.zeros((16, TOK), BF16)

    loads[0].start()

    loads[0].wait()
    group_cells = 8 * dim

    @pl.loop(0, BLK // 8)
    def _(i):
        some = p1[pl.ds(i * group_cells, group_cells)].reshape(8, nb, BLK)
        pw[:, pl.ds(pl.multiple_of(i * 8, 8), 8), :] = jnp.swapaxes(some, 0, 1)

    pair = lambda cc: pl.ds(half_y * cc, half_y)
    def own_quad():
        for yy in range(NY):
            for cc in range(CORES):
                remote = (yy != y) | (cc != c)
                half = rbuf.at[x, z, yy, pl.ds(cc * 64, 64)]

                @pl.when(remote)
                def _(yy=yy, cc=cc, half=half):
                    arrive(half, r_ry.at[yy, cc])

        pltpu.make_async_copy(h_in, rbuf.at[x, z, y, own_half], self_sem.at[0]).wait()

    def z_quad(r):
        out = []
        if r == 0:
            return [(0, z)]
        if r <= longs:
            out.append((2 * r - 1, zw(z - sig * r)))
        if r <= shorts:
            out.append((2 * r, zw(z + sig * r)))
        return out

    def round_a(r):
        for idx, zq in z_quad(r):
            ref = rbuf.at[x, zq, pair(c)]
            if r > 0:
                arrive(ref, r_rz.at[idx])
            is_long = r == 0 or idx % 2 == 1
            is_short = r == 0 or idx % 2 == 0
            if is_long and r < longs:
                send_later(ref, ref, s_rz.at[2 * r + 1], r_rz.at[2 * r + 1], x, z_long)
            if is_short and r < shorts:
                send_later(ref, ref, s_rz.at[2 * r + 2], r_rz.at[2 * r + 2], x, z_short)
            send_later(ref, ref, s_r1.at[idx, 0], r_r1.at[idx, 0], x_up, f)
            send_later(ref, ref, s_r1.at[idx, 1], r_r1.at[idx, 1], x_down, f)
            if r >= DIRECT:
                send_later(ref, ref, s_r2.at[idx, 0], r_r2.at[idx, 0], x_far, f)
            if r > 0:
                send_later(ref, ref, s_rp.at[x, zq], r_rp.at[x, zq], x, partner)

    def round_x1(r):
        for idx, zq in z_quad(r):
            ways = ((x_down, x_up), (x_up, x_down))
            for way, (frm, to) in enumerate(ways):
                arrive(rbuf.at[frm, zq, pair(c)], r_r1.at[idx, way])
                if r < DIRECT:
                    part = rbuf.at[frm, zq, half_y * c + way]
                    send_later(part, part, s_r2.at[idx, way], r_r2.at[idx, way], to, f)
            for frm, _ in ways:
                ref = rbuf.at[frm, zq, pair(c)]
                send_later(ref, ref, s_rp.at[frm, zq], r_rp.at[frm, zq], x, partner)

    def round_x2(r):
        for idx, zq in z_quad(r):
            ref = rbuf.at[x_far, zq, pair(c)]
            if r < DIRECT:
                for way in range(2):
                    arrive(rbuf.at[x_far, zq, half_y * c + way], r_r2.at[idx, way])
            else:
                arrive(ref, r_r2.at[idx, 0])
            send_later(ref, ref, s_rp.at[x_far, zq], r_rp.at[x_far, zq], x, partner)

    own_quad()
    round_a(0)

    lane_row = lax.broadcasted_iota(jnp.int32, (1, BLK), 1)

    def tail_row(ref):
        return jnp.where(lane_row < 64, ref[...].reshape(8, BLK)[0:1], 0.0)

    tail_p = tail_row(p_tail)
    tail_here = jnp.where(
        par == 1, pltpu.roll(jnp.broadcast_to(tail_p, (8, BLK)), 64, 1)[0:1], tail_p
    )

    def window_block(j):
        first = pw[(j - m + nb) % nb]
        second = pw[(j - m - 1 + nb) % nb]
        mixed = pltpu.roll(jnp.where(low, first, second), 64, 1)
        block = jnp.where(par == 1, mixed, first)
        column = j * BLK + lane
        carried = column < 64 * f
        top = jnp.where(carried, 0.0, block)
        bottom = jnp.where(carried, block, 0.0)
        is_tail = (row == BLK - 1) & (column >= 64 * f) & (column < 64 * f + 64)
        bottom = jnp.where(is_tail, tail_here, bottom)
        return jnp.concatenate([top, bottom], axis=0).astype(BF16)

    @pl.loop(0, nz)
    def _(d):
        for hh in range(2):
            for i in range(half_y):
                wins[d, hh, :, i * BLK : (i + 1) * BLK] = window_block((half_y * hh + i) * nz + d)

    for cc, src in enumerate(left_srcs):

        @pl.when(src != f)
        def _(cc=cc):
            arrive(lb.at[x, pl.ds(cc * 64, 64)], r_lf.at[cc])

        @pl.when(src == f)
        def _():
            pltpu.make_async_copy(gq_in, lb.at[x, own_half], self_sem.at[1]).wait()

    @pl.when(has_row)
    def _():
        arrive(rg.at[x], r_lf.at[2])

    for dx in range(1, NX):
        xx = (x + dx) % NX
        send_later(lb.at[x], lb.at[x], s_lx.at[dx - 1, 0], r_lx.at[x, 0], xx, f)
        send_later(rg.at[x], rg.at[x], s_lx.at[dx - 1, 1], r_lx.at[x, 1], xx, f)

    def build_left(xx):
        lt[pl.ds(0, 16), :] = rg[xx].astype(F32)
        lt[pl.ds(16, BLK), :] = lb[xx].astype(F32)
        lt[pl.ds(16 + BLK, 16), :] = rg[xx].astype(F32)
        before = lt[pl.ds(15, BLK), :]
        middle = lt[pl.ds(16, BLK), :]
        after = lt[pl.ds(17, BLK), :]
        zero = jnp.where(h == 0, middle, before)
        one = jnp.where(h == 0, after, middle)
        return zero, one

    zero, one = build_left(x)
    lown[:, pl.ds(0, BLK)] = jnp.transpose(zero).astype(BF16)
    lown[:, pl.ds(BLK, BLK)] = jnp.transpose(one).astype(BF16)

    def partial_chunk(d):
        for mine in range(2):
            hh = c if mine == 0 else 1 - c
            part = jnp.dot(lown[...], wins[d, hh], preferred_element_type=F32)
            for i in range(half_y):
                target = pb if mine == 0 else xs
                target[d, i] = part[:, i * BLK : (i + 1) * BLK]
        send_later(xs.at[d], xr.at[d], s_sp.at[d], r_sp.at[d], x, partner)

    def round_c(r):
        if r >= longs:
            return
        partial_chunk(zw(z + sig * (longs - r)))
        partial_chunk(zw(z - sig * (shorts - r)))

    def chip_sum(d):
        arrive(xr.at[d], r_sp.at[d])
        return pb[d] + xr[d]

    def round_e(r):
        for way, (hops, to, sign) in enumerate(((longs, z_long, 1), (shorts, z_short, -1))):
            if r >= hops:
                continue
            d = zw(z + sig * sign * (hops - r))
            slot = 2 * r + way
            if r == 0:
                pb[d] = chip_sum(d)
                src = pb.at[d]
            else:
                before = slot - 2
                arrive(ring.at[before], r_sr.at[before])
                ring[before] = ring[before] + chip_sum(d)
                src = ring.at[before]
            send_later(src, ring.at[slot], s_sr.at[slot], r_sr.at[slot], x, to)

    def finish_sums():
        total = chip_sum(z)
        slot = 2 * (longs - 1)
        arrive(ring.at[slot], r_sr.at[slot])
        total = total + ring[slot]
        if shorts:
            slot = 2 * (shorts - 1) + 1
            arrive(ring.at[slot], r_sr.at[slot])
            total = total + ring[slot]
        pb[z] = total
        for i in range(half_y):
            for cc in range(CORES):
                yd = half_y * c + i

                @pl.when((yd != y) | (cc != c))
                def _(i=i, cc=cc, yd=yd):
                    send(pb.at[z, i], yb.at[y], s_sy.at[i, cc], r_sy.at[y], x, fid(yd, z, cc))

        @pl.when(h == c)
        def _():
            yb[y] = pb[z, y % half_y]

    def write_cotangents():
        for yy in range(NY):

            @pl.when((yy != y) | (h != c))
            def _(yy=yy):
                arrive(yb.at[yy], r_sy.at[yy])

        for out, base_y in ((gh_out, 0), (ga_out, half_y)):
            total = yb[base_y]
            for i in range(1, half_y):
                total = total + yb[base_y + i]
            total = jnp.transpose(total)
            out[...] = jnp.where(c == 1, total[64:], total[:64]).astype(BF16)

    def full_left():
        for xx in range(NX):

            @pl.when(xx != x)
            def _(xx=xx):
                arrive(lb.at[xx], r_lx.at[xx, 0])
                arrive(rg.at[xx], r_lx.at[xx, 1])

            zero, one = build_left(xx)
            ll[pl.ds(0, BLK), pl.ds(xx * TOK, TOK)] = zero.astype(BF16)
            ll[pl.ds(BLK, BLK), pl.ds(xx * TOK, TOK)] = one.astype(BF16)
        bias_own[...] = lax.dot_general(
            jnp.ones((8, NX * TOK), BF16), ll[pl.ds(0, BLK), :], NT, preferred_element_type=F32
        )

    quarter = nf // 4
    bias_dst = nf // 2 - 1 + f // quarter
    bias_slot = pl.ds(pl.multiple_of((f % quarter) * 8, 8), 8)

    def bias_on():
        @pl.when(f < nf // 2)
        def _():
            send(bias_own, bias_got.at[bias_slot], s_by, r_by, x, bias_dst)

    ext_ref[...] = jnp.zeros((8, BLK), F32)

    def gradient_quad(r):
        for _, zq in z_quad(r):
            for xx in range(NX):
                if r == 0:

                    @pl.when(xx != x)
                    def _(xx=xx, zq=zq):
                        arrive(rbuf.at[xx, zq, pair(1 - c)], r_rp.at[xx, zq])
                else:
                    arrive(rbuf.at[xx, zq, pair(1 - c)], r_rp.at[xx, zq])
            for yy in range(0, NY, 2):
                wide = jnp.concatenate(
                    [
                        jnp.concatenate([rbuf[xx, zq, yy], rbuf[xx, zq, yy + 1]], axis=0)
                        for xx in range(NX)
                    ],
                    axis=1,
                )
                both = lax.dot_general(ll[...], wide, NT, preferred_element_type=F32)
                for i in range(2):
                    j = (yy + i) * nz + zq
                    p_zero = both[:BLK, i * BLK : (i + 1) * BLK]
                    p_one = both[BLK:, i * BLK : (i + 1) * BLK]
                    carried = j * BLK + lane < 64 * f
                    gw[j] = jnp.where(carried, p_one, p_zero)
                    ext_ref[...] = ext_ref[...] + jnp.where(
                        j == m, p_one[BLK - 8 :, :], jnp.zeros((8, BLK), F32)
                    )

    def reorder(zc):
        for yy in range(NY):
            j = yy * nz + zc
            first = gw[j]
            second = gw[(j + 1) % nb]
            mixed = pltpu.roll(jnp.where(low, second, first), 64, 1)
            gb[(j - m + nb) % nb] = jnp.where(par == 1, mixed, first)

    def gradient(r):
        gradient_quad(r)
        if 0 < r <= longs:
            reorder(zw(z - r))
            reorder(zw(z + r - 1))

    bias_add[...] = jnp.zeros((2, nb, BLK), F32)

    def bias_rows():
        half = nb // 2

        @pl.when((f == nf // 2) | (f == nf // 2 - 1))
        def _():
            arrive(bias_got, r_by)
            sums = bias_got[pl.ds(0, half, stride=8), :]

            @pl.when(f == nf // 2)
            def _():
                bias_add[0, pl.ds(0, half)] = sums

            @pl.when(f == nf // 2 - 1)
            def _():
                turned = pltpu.roll(sums, 64, 1)
                index = lax.broadcasted_iota(jnp.int32, (half, BLK), 0)
                before = jnp.where(index == 0, 0.0, pltpu.roll(turned, 1, 0))
                left_half = lax.broadcasted_iota(jnp.int32, (half, BLK), 1) < 64
                bias_add[1, pl.ds(half, half)] = jnp.where(left_half, before, turned)
                ext_ref[...] = ext_ref[...] + sums[half - 1 : half]

    round_c(0)
    round_c(1)
    round_a(1)
    round_e(0)
    round_x1(0)
    round_c(2)
    round_a(2)
    round_x1(1)
    round_x2(0)
    round_c(3)
    full_left()
    loads[1].start()
    loads[2].start()
    round_a(3)
    round_e(1)
    round_x1(2)
    round_x2(1)
    gradient(0)
    round_a(4)
    bias_on()
    round_e(2)
    round_x1(3)
    round_x2(2)
    gradient(1)
    round_x1(4)
    round_x2(3)
    round_e(3)
    gradient(2)
    round_x2(4)
    gradient(3)
    gradient(4)
    bias_rows()

    one_scale = 1.0 / fixes[0]
    two_scale = 1.0 / fixes[1]

    def adam(grad, param, mom_one, mom_two):
        new_one = beta_one * mom_one + (1.0 - beta_one) * grad
        new_two = beta_two * mom_two + (1.0 - beta_two) * grad * grad
        direction = (new_one * one_scale) / (jnp.sqrt(new_two * two_scale) + adam_eps)
        return new_one, new_two, param - learn_rate * (direction + decay_rate * param)

    loads[1].wait()
    loads[2].wait()
    rows_each = 8
    span = rows_each * nb
    steps = BLK // rows_each

    def adam_rows(i, bias_top=None, bias_bottom=None):
        at = pl.ds(pl.multiple_of(i * span, span), span)
        flat = pl.ds(pl.multiple_of(i * span * BLK, span * BLK), span * BLK)
        grad = gb[:, pl.ds(pl.multiple_of(i * rows_each, rows_each), rows_each), :]
        grad = jnp.swapaxes(grad, 0, 1)
        if bias_top is not None:
            grad = jnp.concatenate([grad[:1] + bias_top[None], grad[1:]], axis=0)
        if bias_bottom is not None:
            grad = jnp.concatenate([grad[:-1], grad[-1:] + bias_bottom[None]], axis=0)
        new_one, new_two, updated = adam(
            grad.reshape(span, BLK),
            p1[flat].reshape(span, BLK),
            m1[flat].reshape(span, BLK),
            m2[flat].reshape(span, BLK),
        )
        o1[at, :] = new_one
        o2[at, :] = new_two
        p2[at, :] = updated
        return (updated * updated).reshape(rows_each, nb, BLK)

    acc_ref[...] = jnp.sum(adam_rows(0, bias_top=bias_add[0]), axis=0)

    @pl.loop(1, steps - 1)
    def _(i):
        acc_ref[...] = acc_ref[...] + jnp.sum(adam_rows(i), axis=0)

    squares = adam_rows(steps - 1, bias_bottom=bias_add[1])
    acc_main = acc_ref[...] + jnp.sum(squares[: rows_each - 1], axis=0)
    acc_last = squares[rows_each - 1]
    ext_row = ext_ref[...]
    ext_row = jnp.where(par == 1, pltpu.roll(ext_row, 64, 1), ext_row)[7:8]
    ext_one, ext_two, ext_up = adam(
        ext_row, tail_p, tail_row(m1_tail), tail_row(m2_tail)
    )
    o1[pl.ds(nb * BLK, 8), :] = jnp.broadcast_to(ext_one, (8, BLK))
    o2[pl.ds(nb * BLK, 8), :] = jnp.broadcast_to(ext_two, (8, BLK))
    p2[pl.ds(nb * BLK, 8), :] = jnp.broadcast_to(ext_up, (8, BLK))
    writes = [
        pltpu.make_async_copy(ref, out, out_sem.at[sem])
        for ref, out, sem in ((o1, n1_out, 0), (o2, n2_out, 1), (p2, up_out, 2))
    ]

    heads = lax.broadcasted_iota(jnp.int32, (nb, BLK), 1)
    blocks = lax.broadcasted_iota(jnp.int32, (nb, BLK), 0)
    low_b = heads < 64
    ext_sq = jnp.sum(jnp.where(lane_row < 64, ext_up * ext_up, 0.0), axis=1, keepdims=True)

    def head_of(part):
        spot = f + 2 * blocks + part
        carry = spot // nf
        by_column = (spot % nf) // 2
        main = jnp.where(h == 0, f, by_column)
        last_q = jnp.where(f + carry < nf // 2, f + carry, by_column)
        return main, last_q

    ext_head = jnp.where(f + 1 < nf // 2, f + 1, f // 2)
    total = jnp.where(lane_row == ext_head, ext_sq, 0.0)
    maps = [head_of(0), head_of(1)]
    for part in range(2):
        inside = low_b if part == 0 else jnp.logical_not(low_b)
        for which, acc in enumerate((acc_main, acc_last)):
            sums = jnp.sum(jnp.where(inside, acc, 0.0), axis=1, keepdims=True)
            total = total + jnp.sum(
                jnp.where(maps[part][which] == heads, sums, 0.0), axis=0, keepdims=True
            )
    s_own[...] = total
    offsets = [
        (dy, dz, dc)
        for dy in range(NY)
        for dz in range(nz)
        for dc in range(CORES)
        if (dy, dz, dc) != (0, 0, 0)
    ]
    offsets.sort(key=lambda o: -(min(o[0], NY - o[0]) + min(o[1], nz - o[1])))
    for i, (dy, dz, dc) in enumerate(offsets):
        target = fid((y + dy) % NY, zw(z + dz), (c + dc) % CORES)
        send(s_own, s_grp.at[i], s_sg, r_sg, x, target)
    finish_sums()
    for write in writes:
        write.start()
    arrive(s_grp, r_sg)
    sumsq = s_own[...] + jnp.sum(s_grp[...], axis=0)
    threshold = learn_rate * lasso_weight * math.sqrt(2 * HD * dim + HD)
    shrink = jnp.maximum(1.0 - threshold / jnp.sqrt(sumsq + norm_eps), 0.0)

    def factor(which):
        sides = [
            jnp.sum(jnp.where(maps[part][which] == heads, shrink, 0.0), axis=1, keepdims=True)
            for part in range(2)
        ]
        return jnp.where(low_b, sides[0], sides[1])

    factor_out[pl.ds(0, nb), :] = factor(0)
    factor_out[pl.ds(nb, nb), :] = factor(1)
    ext_shrink = jnp.sum(jnp.where(lane_row == ext_head, shrink, 0.0), axis=1, keepdims=True)
    factor_out[pl.ds(2 * nb, 8), :] = jnp.broadcast_to(ext_shrink, (8, BLK))

    write_cotangents()

    def sent(src, ss):
        pltpu.make_async_remote_copy(
            src_ref=src, dst_ref=src, send_sem=ss, recv_sem=r_by,
            device_id=(x, partner), device_id_type=MESH,
        ).wait_send()

    sent(s_grp, s_sg)
    for copy in pending:
        copy.wait_send()
    for yd, cc, src in right_sends():

        @pl.when((yd != y) | (cc != c))
        def _(yd=yd, cc=cc, src=src):
            sent(src, s_ry.at[yd, cc])

    for i in range(half_y):
        for cc in range(CORES):
            yd = half_y * c + i

            @pl.when((yd != y) | (cc != c))
            def _(i=i, cc=cc):
                sent(pb.at[z, i], s_sy.at[i, cc])

    for i, (src, dst) in enumerate(zip((gq_in, go_in), left_dsts)):

        @pl.when(dst != f)
        def _(i=i, src=src):
            sent(src, s_lf.at[i])

    @pl.when(gives_row)
    def _():
        sent(row_part(gq_in), s_lf.at[2])

    @pl.when(f < nf // 2)
    def _():
        sent(bias_own, s_by)

    for write in writes:
        write.wait()


def finish(nb, gh, ga, up, n1, n2, factors, gh_out, ga_out, np_out, n1_out, n2_out, scaled, sems):
    copies = [
        pltpu.make_async_copy(gh, gh_out, sems.at[6]),
        pltpu.make_async_copy(ga, ga_out, sems.at[7]),
        pltpu.make_async_copy(n1, n1_out, sems.at[0]),
        pltpu.make_async_copy(n2, n2_out, sems.at[1]),
    ]
    for copy in copies:
        copy.start()
    pieces, rows_each = 4, 4
    span = rows_each * nb
    steps = BLK // rows_each // pieces
    main = factors[pl.ds(0, nb), :]
    for piece in range(pieces):
        start = piece * steps * span
        full = steps - 1 if piece == pieces - 1 else steps

        @pl.loop(0, full)
        def _(i):
            at = pl.ds(pl.multiple_of(start + i * span, span), span)
            block = up[at, :].reshape(rows_each, nb, BLK) * factors[pl.ds(0, nb), :][None]
            scaled[at, :] = block.reshape(span, BLK)

        rows = steps * span
        if piece == pieces - 1:
            at = pl.ds(start + full * span, span - nb)
            block = up[at, :].reshape(rows_each - 1, nb, BLK) * main[None]
            scaled[at, :] = block.reshape(span - nb, BLK)
            at = pl.ds(nb * BLK - nb, nb)
            scaled[at, :] = up[at, :] * factors[pl.ds(nb, nb), :]
            at = pl.ds(nb * BLK, 8)
            scaled[at, :] = up[at, :] * factors[pl.ds(2 * nb, 8), :]
            rows += 8
        at = pl.ds(start, rows)
        copy = pltpu.make_async_copy(scaled.at[at], np_out.at[at], sems.at[2 + piece])
        copy.start()
        copies.append(copy)
    for copy in copies:
        copy.wait()


def on_device(
    nz, hidden, grad_query, attn_out, grad_output, flat_params, moment_one, moment_two, step_count
):
    nb = NY * nz
    cells = nb * BLK * BLK
    rows = nb * BLK
    shard_len = flat_params.shape[0]
    step_num = step_count[0].astype(F32)
    fixes = jnp.stack(
        [
            1.0 - jnp.power(jnp.float32(beta_one), step_num),
            1.0 - jnp.power(jnp.float32(beta_two), step_num),
        ]
    )
    vm = lambda shape, dtype=F32: pltpu.VMEM(shape, dtype)
    dma = lambda *shape: pltpu.SemaphoreType.DMA(shape) if shape else pltpu.SemaphoreType.DMA
    grp = nz * CORES
    whole = pl.BlockSpec(memory_space=pltpu.VMEM)
    anywhere = pl.BlockSpec(memory_space=pl.ANY)
    scratch = [
        vm((cells,)), vm((cells,)), vm((cells,)),
        vm((rows + 8, BLK)), vm((rows + 8, BLK)), vm((rows + 8, BLK)),
        vm((nb, BLK, BLK)), vm((nb, BLK, BLK)), vm((nb, BLK, BLK)),
        vm((NX, BLK, TOK), BF16), vm((NX, 16, TOK), BF16),
        vm((BLK + 32, TOK)), vm((2 * BLK, NX * TOK), BF16), vm((TOK, 2 * BLK), BF16),
        vm((nz, 2, 2 * BLK, NY // 2 * BLK), BF16), vm((NX, nz, NY, TOK, BLK), BF16),
        vm((nz, NY // 2, TOK, BLK)), vm((nz, NY // 2, TOK, BLK)), vm((nz, NY // 2, TOK, BLK)),
        vm((nz, NY // 2, TOK, BLK)), vm((NY, TOK, BLK)),
        vm((8, BLK)), vm((grp * 8, BLK)), vm((2, nb, BLK)),
        vm((8, BLK)), vm((nb, BLK)),
        vm((1, BLK)), vm((NY * grp - 1, 1, BLK)),
        dma(3), dma(3), dma(2), dma(NY, CORES), dma(NY, CORES), dma(3), dma(3),
        dma(NX - 1, 2), dma(NX, 2),
        dma(), dma(), dma(nz), dma(nz), dma(nz, 2), dma(nz, 2),
        dma(nz, 2), dma(nz, 2), dma(NX, nz), dma(NX, nz),
        dma(nz), dma(nz), dma(nz), dma(nz), dma(NY // 2, CORES), dma(NY),
        dma(), dma(),
    ]
    cotangent = jax.ShapeDtypeStruct((64, TOK), BF16)
    flat = jax.ShapeDtypeStruct((rows + 8, BLK), F32)
    tail = pl.BlockSpec((1024,), lambda i: (cells // 1024,))
    outs = pl.pallas_call(
        functools.partial(kernel, nz),
        grid=(1,),
        out_shape=[
            cotangent, cotangent,
            flat, flat, flat,
            jax.ShapeDtypeStruct((2 * nb + 8, BLK), F32),
        ],
        in_specs=[anywhere] + [tail] * 3 + [pl.BlockSpec(memory_space=pltpu.SMEM)] + [anywhere] * 3,
        out_specs=[whole] * 2 + [anywhere] * 3 + [whole],
        scratch_shapes=scratch,
        compiler_params=pltpu.CompilerParams(
            collective_id=0, has_side_effects=True, vmem_limit_bytes=46 * 1024 * 1024
        ),
        cost_estimate=pl.CostEstimate(
            flops=4 * 512 * 128 * 4096, bytes_accessed=6 * 2 * 1024 * 1024, transcendentals=524352
        ),
        name="step",
    )(
        jnp.stack([hidden.T, grad_query.T, attn_out.T, grad_output.T]),
        flat_params, moment_one, moment_two, fixes, flat_params, moment_one, moment_two,
    )
    results = pl.pallas_call(
        functools.partial(finish, nb),
        out_shape=[cotangent] * 2 + [flat] * 3,
        in_specs=[anywhere, anywhere, whole, anywhere, anywhere, whole],
        out_specs=[anywhere] * 5,
        scratch_shapes=[vm((rows + 8, BLK)), dma(8)],
        compiler_params=pltpu.CompilerParams(vmem_limit_bytes=16 * 1024 * 1024),
        name="finish",
    )(*outs)
    grad_hidden, grad_attn = results[0].T, results[1].T
    new_params, new_one, new_two = (part.reshape(-1)[:shard_len] for part in results[2:])
    return (grad_hidden, grad_attn, new_params, new_one, new_two)


def solution(mesh):
    nz = mesh.shape["fsdp"] // (NY * CORES)
    in_specs = (
        P("dp", "fsdp"),
        P("dp", "fsdp"),
        P("dp", "fsdp"),
        P("dp", "fsdp"),
        P("fsdp"),
        P("fsdp"),
        P("fsdp"),
        P(),
    )
    out_specs = (P("dp", "fsdp"), P("dp", "fsdp"), P("fsdp"), P("fsdp"), P("fsdp"))
    return jax.shard_map(
        functools.partial(on_device, nz), mesh=mesh, in_specs=in_specs, out_specs=out_specs, check_vma=False
    )
```

```python
import functools
import math

import jax
import jax.numpy as jnp
from jax import lax
from jax.experimental import pallas as pl
from jax.experimental.pallas import tpu as pltpu
from jax.sharding import PartitionSpec as P

HD = 128
NX = 4
NY = 4
CORES = 2
TOK = 128
BLK = 128
DIRECT = 4

beta_one = 0.9
beta_two = 0.95
adam_eps = 1e-08
learn_rate = 0.02
decay_rate = 0.1
lasso_weight = 2.0
norm_eps = 1e-06

MESH = pl.DeviceIdType.MESH
F32 = jnp.float32
BF16 = jnp.bfloat16
NT = (((1,), (1,)), ((), ()))


def kernel(
    nz, acts, p_tail, m1_tail, m2_tail, fixes, p_hbm, m1_hbm, m2_hbm,
    gh_out, ga_out, up_out, n1_out, n2_out, factor_out,
    p1, m1, m2, p2, o1, o2, pw, m1w, m2w, gw, edge_in, gedge,
    lb, rg, lt, ll, lown,
    wins, rbuf, pb, xs, xr, ring, yb, bias_own, bias_got, bias_add,
    ext_ref, acc_ref, s_own, s_grp,
    in_sem, out_sem, self_sem, s_ry, r_ry, s_lf, r_lf, s_lx, r_lx,
    s_by, r_by, s_rz, r_rz, s_r1, r_r1, s_r2, r_r2, s_rp, r_rp,
    s_sp, r_sp, s_sr, r_sr, s_sy, r_sy, s_sg, r_sg,
):
    h_in, gq_in, a_in, go_in = (acts.at[i] for i in range(4))
    nf = NY * nz * CORES
    nb = NY * nz
    dim = nb * BLK
    half_y = NY // 2
    longs, shorts = nz // 2, nz - 1 - nz // 2
    x = lax.axis_index("dp")
    f = lax.axis_index("fsdp")
    c = f % CORES
    z = (f // CORES) % nz
    y = f // (CORES * nz)
    h = y // half_y
    m = f // 2
    par = f % 2
    k = f // CORES
    sig = 1 - 2 * c

    def fid(yy, zz, cc):
        return (yy * nz + zz) * CORES + cc

    def zw(v):
        return (v + 2 * nz) % nz

    partner = fid(y, z, 1 - c)
    z_long = fid(y, zw(z + sig), c)
    z_short = fid(y, zw(z - sig), c)
    x_up = (x + 1) % NX
    x_down = (x + NX - 1) % NX
    x_far = (x + 2) % NX

    pending = []

    def send(src, dst, ss, rs, xx, ff):
        copy = pltpu.make_async_remote_copy(
            src_ref=src, dst_ref=dst, send_sem=ss, recv_sem=rs,
            device_id=(xx, ff), device_id_type=MESH,
        )
        copy.start()
        return copy

    def send_later(*args):
        pending.append(send(*args))

    def arrive(dst, rs):
        pltpu.make_async_remote_copy(
            src_ref=dst, dst_ref=dst, send_sem=s_by, recv_sem=rs,
            device_id=(x, partner), device_id_type=MESH,
        ).wait_recv()

    cells = nb * BLK * BLK
    loads = [
        pltpu.make_async_copy(src.at[pl.ds(0, cells)], dst, in_sem.at[i])
        for i, (src, dst) in enumerate(((p_hbm, p1), (m1_hbm, m1), (m2_hbm, m2)))
    ]

    barrier = pltpu.get_barrier_semaphore()

    def greet(xx, ff):
        pl.semaphore_signal(barrier, inc=1, device_id=(xx, ff), device_id_type=MESH)

    near_z = sorted({1, nz - 1})
    for dz in near_z:
        greet(x, fid(y, zw(z + dz), c))
    greet(x, partner)
    for dy in range(1, NY):
        for dc in range(CORES):
            greet(x, fid((y + dy) % NY, z, (c + dc) % CORES))
    for dx in range(1, NX):
        greet((x + dx) % NX, f)
    fl = f % (nf // 2)
    row_src = 2 * (fl + 1 - 2 * h) + h
    row_chip = fl + 1 - 2 * h
    has_row = (row_chip >= 0) & (row_chip < nf // 2)
    left_dsts = (k, nf // 2 + k)
    left_srcs = (2 * fl, 2 * fl + 1)
    row_dst_low = k - 1 + 2 * c
    gives_row = (row_dst_low >= 0) & (row_dst_low < nf // 2)
    row_dst = c * (nf // 2) + row_dst_low

    for src in left_srcs:

        @pl.when(src != f)
        def _(src=src):
            greet(x, src)

    @pl.when(has_row)
    def _():
        greet(x, row_src)

    greeted = len(near_z) + 1 + (NY - 1) * CORES + NX - 1
    for dst in left_dsts:
        greeted = greeted + (dst != f).astype(jnp.int32)
    greeted = greeted + gives_row.astype(jnp.int32)
    lane = lax.broadcasted_iota(jnp.int32, (BLK, BLK), 1)
    row = lax.broadcasted_iota(jnp.int32, (BLK, BLK), 0)
    low = lane < 64

    pl.semaphore_wait(barrier, greeted)

    own_half = pl.ds(pl.multiple_of(c * 64, 64), 64)

    def right_sends():
        for yd in range(NY):
            src = h_in if yd < half_y else a_in
            for cc in range(CORES):
                yield yd, cc, src

    for yd, cc, src in right_sends():
        remote = (yd != y) | (cc != c)

        @pl.when(remote)
        def _(yd=yd, cc=cc, src=src):
            send(
                src, rbuf.at[x, z, y, own_half], s_ry.at[yd, cc], r_ry.at[y, c], x, fid(yd, z, cc)
            )

        @pl.when(jnp.logical_not(remote))
        def _(src=src):
            pltpu.make_async_copy(src, rbuf.at[x, z, y, own_half], self_sem.at[0]).start()

    row_part = lambda src: src.at[pl.ds(pl.multiple_of(c * (64 - 16), 16), 16)]
    for i, (src, dst) in enumerate(zip((gq_in, go_in), left_dsts)):

        @pl.when(dst != f)
        def _(i=i, src=src, dst=dst):
            send(src, lb.at[x, own_half], s_lf.at[i], r_lf.at[c], x, dst)

        @pl.when(dst == f)
        def _(src=src):
            pltpu.make_async_copy(src, lb.at[x, own_half], self_sem.at[1]).start()

        @pl.when(gives_row & (c == i))
        def _(src=src):
            send(row_part(src), rg.at[x], s_lf.at[2], r_lf.at[2], x, row_dst)

    @pl.when(jnp.logical_not(has_row))
    def _():
        rg[x] = jnp.zeros((16, TOK), BF16)

    loads[0].start()

    loads[0].wait()
    group_cells = 8 * dim

    @pl.loop(0, BLK // 8)
    def _(i):
        some = p1[pl.ds(i * group_cells, group_cells)].reshape(8, nb, BLK)
        pw[:, pl.ds(pl.multiple_of(i * 8, 8), 8), :] = jnp.swapaxes(some, 0, 1)

    pair = lambda cc: pl.ds(half_y * cc, half_y)
    def own_quad():
        for yy in range(NY):
            for cc in range(CORES):
                remote = (yy != y) | (cc != c)
                half = rbuf.at[x, z, yy, pl.ds(cc * 64, 64)]

                @pl.when(remote)
                def _(yy=yy, cc=cc, half=half):
                    arrive(half, r_ry.at[yy, cc])

        pltpu.make_async_copy(h_in, rbuf.at[x, z, y, own_half], self_sem.at[0]).wait()

    def z_quad(r):
        out = []
        if r == 0:
            return [(0, z)]
        if r <= longs:
            out.append((2 * r - 1, zw(z - sig * r)))
        if r <= shorts:
            out.append((2 * r, zw(z + sig * r)))
        return out

    def round_a(r):
        for idx, zq in z_quad(r):
            ref = rbuf.at[x, zq, pair(c)]
            if r > 0:
                arrive(ref, r_rz.at[idx])
            is_long = r == 0 or idx % 2 == 1
            is_short = r == 0 or idx % 2 == 0
            if is_long and r < longs:
                send_later(ref, ref, s_rz.at[2 * r + 1], r_rz.at[2 * r + 1], x, z_long)
            if is_short and r < shorts:
                send_later(ref, ref, s_rz.at[2 * r + 2], r_rz.at[2 * r + 2], x, z_short)
            send_later(ref, ref, s_r1.at[idx, 0], r_r1.at[idx, 0], x_up, f)
            send_later(ref, ref, s_r1.at[idx, 1], r_r1.at[idx, 1], x_down, f)
            if r >= DIRECT:
                send_later(ref, ref, s_r2.at[idx, 0], r_r2.at[idx, 0], x_far, f)
            if r > 0:
                send_later(ref, ref, s_rp.at[x, zq], r_rp.at[x, zq], x, partner)

    def round_x1(r):
        for idx, zq in z_quad(r):
            ways = ((x_down, x_up), (x_up, x_down))
            for way, (frm, to) in enumerate(ways):
                arrive(rbuf.at[frm, zq, pair(c)], r_r1.at[idx, way])
                if r < DIRECT:
                    part = rbuf.at[frm, zq, half_y * c + way]
                    send_later(part, part, s_r2.at[idx, way], r_r2.at[idx, way], to, f)
            for frm, _ in ways:
                ref = rbuf.at[frm, zq, pair(c)]
                send_later(ref, ref, s_rp.at[frm, zq], r_rp.at[frm, zq], x, partner)

    def round_x2(r):
        for idx, zq in z_quad(r):
            ref = rbuf.at[x_far, zq, pair(c)]
            if r < DIRECT:
                for way in range(2):
                    arrive(rbuf.at[x_far, zq, half_y * c + way], r_r2.at[idx, way])
            else:
                arrive(ref, r_r2.at[idx, 0])
            send_later(ref, ref, s_rp.at[x_far, zq], r_rp.at[x_far, zq], x, partner)

    own_quad()
    round_a(0)

    lane_row = lax.broadcasted_iota(jnp.int32, (1, BLK), 1)

    def tail_row(ref):
        return jnp.where(lane_row < 64, ref[...].reshape(8, BLK)[0:1], 0.0)

    tail_p = tail_row(p_tail)
    tail_here = jnp.where(
        par == 1, pltpu.roll(jnp.broadcast_to(tail_p, (8, BLK)), 64, 1)[0:1], tail_p
    )

    def window_block(j):
        first = pw[(j - m + nb) % nb]
        second = pw[(j - m - 1 + nb) % nb]
        mixed = pltpu.roll(jnp.where(low, first, second), 64, 1)
        block = jnp.where(par == 1, mixed, first)
        column = j * BLK + lane
        carried = column < 64 * f
        top = jnp.where(carried, 0.0, block)
        bottom = jnp.where(carried, block, 0.0)
        is_tail = (row == BLK - 1) & (column >= 64 * f) & (column < 64 * f + 64)
        bottom = jnp.where(is_tail, tail_here, bottom)
        return jnp.concatenate([top, bottom], axis=0).astype(BF16)

    @pl.loop(0, nz)
    def _(d):
        for hh in range(2):
            for i in range(half_y):
                wins[d, hh, :, i * BLK : (i + 1) * BLK] = window_block((half_y * hh + i) * nz + d)

    for cc, src in enumerate(left_srcs):

        @pl.when(src != f)
        def _(cc=cc):
            arrive(lb.at[x, pl.ds(cc * 64, 64)], r_lf.at[cc])

        @pl.when(src == f)
        def _():
            pltpu.make_async_copy(gq_in, lb.at[x, own_half], self_sem.at[1]).wait()

    @pl.when(has_row)
    def _():
        arrive(rg.at[x], r_lf.at[2])

    for dx in range(1, NX):
        xx = (x + dx) % NX
        send_later(lb.at[x], lb.at[x], s_lx.at[dx - 1, 0], r_lx.at[x, 0], xx, f)
        send_later(rg.at[x], rg.at[x], s_lx.at[dx - 1, 1], r_lx.at[x, 1], xx, f)

    def build_left(xx):
        lt[pl.ds(0, 16), :] = rg[xx].astype(F32)
        lt[pl.ds(16, BLK), :] = lb[xx].astype(F32)
        lt[pl.ds(16 + BLK, 16), :] = rg[xx].astype(F32)
        before = lt[pl.ds(15, BLK), :]
        middle = lt[pl.ds(16, BLK), :]
        after = lt[pl.ds(17, BLK), :]
        zero = jnp.where(h == 0, middle, before)
        one = jnp.where(h == 0, after, middle)
        return zero, one

    zero, one = build_left(x)
    lown[:, pl.ds(0, BLK)] = jnp.transpose(zero).astype(BF16)
    lown[:, pl.ds(BLK, BLK)] = jnp.transpose(one).astype(BF16)

    def partial_chunk(d):
        for mine in range(2):
            hh = c if mine == 0 else 1 - c
            part = jnp.dot(lown[...], wins[d, hh], preferred_element_type=F32)
            for i in range(half_y):
                target = pb if mine == 0 else xs
                target[d, i] = part[:, i * BLK : (i + 1) * BLK]
        send_later(xs.at[d], xr.at[d], s_sp.at[d], r_sp.at[d], x, partner)

    def round_c(r):
        if r >= longs:
            return
        partial_chunk(zw(z + sig * (longs - r)))
        partial_chunk(zw(z - sig * (shorts - r)))

    def chip_sum(d):
        arrive(xr.at[d], r_sp.at[d])
        return pb[d] + xr[d]

    def round_e(r):
        for way, (hops, to, sign) in enumerate(((longs, z_long, 1), (shorts, z_short, -1))):
            if r >= hops:
                continue
            d = zw(z + sig * sign * (hops - r))
            slot = 2 * r + way
            if r == 0:
                pb[d] = chip_sum(d)
                src = pb.at[d]
            else:
                before = slot - 2
                arrive(ring.at[before], r_sr.at[before])
                ring[before] = ring[before] + chip_sum(d)
                src = ring.at[before]
            send_later(src, ring.at[slot], s_sr.at[slot], r_sr.at[slot], x, to)

    def finish_sums():
        total = chip_sum(z)
        slot = 2 * (longs - 1)
        arrive(ring.at[slot], r_sr.at[slot])
        total = total + ring[slot]
        if shorts:
            slot = 2 * (shorts - 1) + 1
            arrive(ring.at[slot], r_sr.at[slot])
            total = total + ring[slot]
        pb[z] = total
        for i in range(half_y):
            for cc in range(CORES):
                yd = half_y * c + i

                @pl.when((yd != y) | (cc != c))
                def _(i=i, cc=cc, yd=yd):
                    send(pb.at[z, i], yb.at[y], s_sy.at[i, cc], r_sy.at[y], x, fid(yd, z, cc))

        @pl.when(h == c)
        def _():
            yb[y] = pb[z, y % half_y]

    def write_cotangents():
        for yy in range(NY):

            @pl.when((yy != y) | (h != c))
            def _(yy=yy):
                arrive(yb.at[yy], r_sy.at[yy])

        for out, base_y in ((gh_out, 0), (ga_out, half_y)):
            total = yb[base_y]
            for i in range(1, half_y):
                total = total + yb[base_y + i]
            total = jnp.transpose(total)
            out[...] = jnp.where(c == 1, total[64:], total[:64]).astype(BF16)

    def full_left():
        for xx in range(NX):

            @pl.when(xx != x)
            def _(xx=xx):
                arrive(lb.at[xx], r_lx.at[xx, 0])
                arrive(rg.at[xx], r_lx.at[xx, 1])

            zero, one = build_left(xx)
            ll[pl.ds(0, BLK), pl.ds(xx * TOK, TOK)] = zero.astype(BF16)
            ll[pl.ds(BLK, BLK), pl.ds(xx * TOK, TOK)] = one.astype(BF16)
        bias_own[...] = lax.dot_general(
            jnp.ones((8, NX * TOK), BF16), ll[pl.ds(0, BLK), :], NT, preferred_element_type=F32
        )

    quarter = nf // 4
    bias_dst = nf // 2 - 1 + f // quarter
    bias_slot = pl.ds(pl.multiple_of((f % quarter) * 8, 8), 8)

    def bias_on():
        @pl.when(f < nf // 2)
        def _():
            send(bias_own, bias_got.at[bias_slot], s_by, r_by, x, bias_dst)

    ext_ref[...] = jnp.zeros((8, BLK), F32)

    def gradient_quad(r):
        for _, zq in z_quad(r):
            for xx in range(NX):
                if r == 0:

                    @pl.when(xx != x)
                    def _(xx=xx, zq=zq):
                        arrive(rbuf.at[xx, zq, pair(1 - c)], r_rp.at[xx, zq])
                else:
                    arrive(rbuf.at[xx, zq, pair(1 - c)], r_rp.at[xx, zq])
            for yy in range(0, NY, 2):
                wide = jnp.concatenate(
                    [
                        jnp.concatenate([rbuf[xx, zq, yy], rbuf[xx, zq, yy + 1]], axis=0)
                        for xx in range(NX)
                    ],
                    axis=1,
                )
                both = lax.dot_general(ll[...], wide, NT, preferred_element_type=F32)
                for i in range(2):
                    j = (yy + i) * nz + zq
                    p_zero = both[:BLK, i * BLK : (i + 1) * BLK]
                    p_one = both[BLK:, i * BLK : (i + 1) * BLK]
                    carried = j * BLK + lane < 64 * f
                    gw[j] = jnp.where(carried, p_one, p_zero)
                    ext_ref[...] = ext_ref[...] + jnp.where(
                        j == m, p_one[BLK - 8 :, :], jnp.zeros((8, BLK), F32)
                    )

    one_scale = 1.0 / fixes[0]
    two_scale = 1.0 / fixes[1]

    def adam(grad, param, mom_one, mom_two):
        new_one = beta_one * mom_one + (1.0 - beta_one) * grad
        new_two = beta_two * mom_two + (1.0 - beta_two) * grad * grad
        direction = (new_one * one_scale) / (jnp.sqrt(new_two * two_scale) + adam_eps)
        return new_one, new_two, param - learn_rate * (direction + decay_rate * param)

    rows_each = 8
    span = rows_each * nb

    def by_block(source, target):
        @pl.loop(0, BLK // rows_each)
        def _(i):
            flat = pl.ds(pl.multiple_of(i * span * BLK, span * BLK), span * BLK)
            some = source[flat].reshape(rows_each, nb, BLK)
            at = pl.ds(pl.multiple_of(i * rows_each, rows_each), rows_each)
            target[:, at, :] = jnp.swapaxes(some, 0, 1)

    def moments():
        loads[1].wait()
        loads[2].wait()
        by_block(m1, m1w)
        by_block(m2, m2w)
        for n, ref in enumerate((pw, m1w, m2w)):
            edge_in[n, 0] = jnp.swapaxes(ref[:, pl.ds(0, 8), :], 0, 1)[0]
            edge_in[n, 1] = jnp.swapaxes(ref[:, pl.ds(BLK - 8, 8), :], 0, 1)[7]

    inner = (row > 0) & (row < BLK - 1)

    def adam_blocks(zc):
        for yy in range(NY):
            j = yy * nz + zc
            first = gw[j]
            second = gw[(j + 1) % nb]
            mixed = pltpu.roll(jnp.where(low, second, first), 64, 1)
            grad = jnp.where(par == 1, mixed, first)
            b = (j - m + nb) % nb
            new_one, new_two, updated = adam(grad, pw[b], m1w[b], m2w[b])
            m1w[b] = new_one
            m2w[b] = new_two
            pw[b] = updated
            squares = jnp.where(inner, updated * updated, 0.0)
            acc_ref[pl.ds(b, 1), :] = jnp.sum(squares, axis=0, keepdims=True)
            gedge[0, pl.ds(b, 1), :] = grad[:1]
            gedge[1, pl.ds(b, 1), :] = grad[BLK - 1 :]

    def gradient(r):
        gradient_quad(r)
        if 0 < r <= longs:
            adam_blocks(zw(z - r))
            adam_blocks(zw(z + r - 1))

    bias_add[...] = jnp.zeros((2, nb, BLK), F32)

    def bias_rows():
        half = nb // 2

        @pl.when((f == nf // 2) | (f == nf // 2 - 1))
        def _():
            arrive(bias_got, r_by)
            sums = bias_got[pl.ds(0, half, stride=8), :]

            @pl.when(f == nf // 2)
            def _():
                bias_add[0, pl.ds(0, half)] = sums

            @pl.when(f == nf // 2 - 1)
            def _():
                turned = pltpu.roll(sums, 64, 1)
                index = lax.broadcasted_iota(jnp.int32, (half, BLK), 0)
                before = jnp.where(index == 0, 0.0, pltpu.roll(turned, 1, 0))
                left_half = lax.broadcasted_iota(jnp.int32, (half, BLK), 1) < 64
                bias_add[1, pl.ds(half, half)] = jnp.where(left_half, before, turned)
                ext_ref[...] = ext_ref[...] + sums[half - 1 : half]

    round_c(0)
    round_c(1)
    round_a(1)
    round_e(0)
    round_x1(0)
    round_c(2)
    round_a(2)
    round_x1(1)
    round_x2(0)
    round_c(3)
    full_left()
    loads[1].start()
    loads[2].start()
    round_a(3)
    round_e(1)
    round_x1(2)
    round_x2(1)
    moments()
    gradient(0)
    round_a(4)
    bias_on()
    round_e(2)
    round_x1(3)
    round_x2(2)
    gradient(1)
    round_x1(4)
    round_x2(3)
    round_e(3)
    gradient(2)
    round_x2(4)
    gradient(3)
    gradient(4)
    bias_rows()

    def edge_step(e):
        return adam(gedge[e] + bias_add[e], edge_in[0, e], edge_in[1, e], edge_in[2, e])

    edges = [edge_step(e) for e in range(2)]
    acc_main = acc_ref[...] + edges[0][2] * edges[0][2]
    acc_last = edges[1][2] * edges[1][2]
    ext_row = ext_ref[...]
    ext_row = jnp.where(par == 1, pltpu.roll(ext_row, 64, 1), ext_row)[7:8]
    ext_one, ext_two, ext_up = adam(
        ext_row, tail_p, tail_row(m1_tail), tail_row(m2_tail)
    )
    o1[pl.ds(nb * BLK, 8), :] = jnp.broadcast_to(ext_one, (8, BLK))
    o2[pl.ds(nb * BLK, 8), :] = jnp.broadcast_to(ext_two, (8, BLK))
    p2[pl.ds(nb * BLK, 8), :] = jnp.broadcast_to(ext_up, (8, BLK))
    writes = [
        pltpu.make_async_copy(ref, out, out_sem.at[sem])
        for ref, out, sem in ((o1, n1_out, 0), (o2, n2_out, 1), (p2, up_out, 2))
    ]

    heads = lax.broadcasted_iota(jnp.int32, (nb, BLK), 1)
    blocks = lax.broadcasted_iota(jnp.int32, (nb, BLK), 0)
    low_b = heads < 64
    ext_sq = jnp.sum(jnp.where(lane_row < 64, ext_up * ext_up, 0.0), axis=1, keepdims=True)

    def head_of(part):
        spot = f + 2 * blocks + part
        carry = spot // nf
        by_column = (spot % nf) // 2
        main = jnp.where(h == 0, f, by_column)
        last_q = jnp.where(f + carry < nf // 2, f + carry, by_column)
        return main, last_q

    ext_head = jnp.where(f + 1 < nf // 2, f + 1, f // 2)
    total = jnp.where(lane_row == ext_head, ext_sq, 0.0)
    maps = [head_of(0), head_of(1)]
    for part in range(2):
        inside = low_b if part == 0 else jnp.logical_not(low_b)
        for which, acc in enumerate((acc_main, acc_last)):
            sums = jnp.sum(jnp.where(inside, acc, 0.0), axis=1, keepdims=True)
            total = total + jnp.sum(
                jnp.where(maps[part][which] == heads, sums, 0.0), axis=0, keepdims=True
            )
    s_own[...] = total
    offsets = [
        (dy, dz, dc)
        for dy in range(NY)
        for dz in range(nz)
        for dc in range(CORES)
        if (dy, dz, dc) != (0, 0, 0)
    ]
    offsets.sort(key=lambda o: -(min(o[0], NY - o[0]) + min(o[1], nz - o[1])))
    for i, (dy, dz, dc) in enumerate(offsets):
        target = fid((y + dy) % NY, zw(z + dz), (c + dc) % CORES)
        send(s_own, s_grp.at[i], s_sg, r_sg, x, target)
    finish_sums()
    for n, (blocked, flat) in enumerate(((m1w, o1), (m2w, o2), (pw, p2))):

        @pl.loop(0, BLK // rows_each)
        def _(i):
            some = blocked[:, pl.ds(pl.multiple_of(i * rows_each, rows_each), rows_each), :]
            at = pl.ds(pl.multiple_of(i * span, span), span)
            flat[at, :] = jnp.swapaxes(some, 0, 1).reshape(span, BLK)

        flat[pl.ds(0, nb), :] = edges[0][n]
        flat[pl.ds((BLK - 1) * nb, nb), :] = edges[1][n]
        writes[n].start()

    arrive(s_grp, r_sg)
    sumsq = s_own[...] + jnp.sum(s_grp[...], axis=0)
    threshold = learn_rate * lasso_weight * math.sqrt(2 * HD * dim + HD)
    shrink = jnp.maximum(1.0 - threshold / jnp.sqrt(sumsq + norm_eps), 0.0)

    def factor(which):
        sides = [
            jnp.sum(jnp.where(maps[part][which] == heads, shrink, 0.0), axis=1, keepdims=True)
            for part in range(2)
        ]
        return jnp.where(low_b, sides[0], sides[1])

    factor_out[pl.ds(0, nb), :] = factor(0)
    factor_out[pl.ds(nb, nb), :] = factor(1)
    ext_shrink = jnp.sum(jnp.where(lane_row == ext_head, shrink, 0.0), axis=1, keepdims=True)
    factor_out[pl.ds(2 * nb, 8), :] = jnp.broadcast_to(ext_shrink, (8, BLK))

    write_cotangents()

    def sent(src, ss):
        pltpu.make_async_remote_copy(
            src_ref=src, dst_ref=src, send_sem=ss, recv_sem=r_by,
            device_id=(x, partner), device_id_type=MESH,
        ).wait_send()

    sent(s_grp, s_sg)
    for copy in pending:
        copy.wait_send()
    for yd, cc, src in right_sends():

        @pl.when((yd != y) | (cc != c))
        def _(yd=yd, cc=cc, src=src):
            sent(src, s_ry.at[yd, cc])

    for i in range(half_y):
        for cc in range(CORES):
            yd = half_y * c + i

            @pl.when((yd != y) | (cc != c))
            def _(i=i, cc=cc):
                sent(pb.at[z, i], s_sy.at[i, cc])

    for i, (src, dst) in enumerate(zip((gq_in, go_in), left_dsts)):

        @pl.when(dst != f)
        def _(i=i, src=src):
            sent(src, s_lf.at[i])

    @pl.when(gives_row)
    def _():
        sent(row_part(gq_in), s_lf.at[2])

    @pl.when(f < nf // 2)
    def _():
        sent(bias_own, s_by)

    for write in writes:
        write.wait()


def finish(nb, gh, ga, up, n1, n2, factors, gh_out, ga_out, np_out, n1_out, n2_out, scaled, sems):
    copies = [
        pltpu.make_async_copy(gh, gh_out, sems.at[6]),
        pltpu.make_async_copy(ga, ga_out, sems.at[7]),
        pltpu.make_async_copy(n1, n1_out, sems.at[0]),
        pltpu.make_async_copy(n2, n2_out, sems.at[1]),
    ]
    for copy in copies:
        copy.start()
    pieces, rows_each = 4, 4
    span = rows_each * nb
    steps = BLK // rows_each // pieces
    main = factors[pl.ds(0, nb), :]
    for piece in range(pieces):
        start = piece * steps * span
        full = steps - 1 if piece == pieces - 1 else steps

        @pl.loop(0, full)
        def _(i):
            at = pl.ds(pl.multiple_of(start + i * span, span), span)
            block = up[at, :].reshape(rows_each, nb, BLK) * factors[pl.ds(0, nb), :][None]
            scaled[at, :] = block.reshape(span, BLK)

        rows = steps * span
        if piece == pieces - 1:
            at = pl.ds(start + full * span, span - nb)
            block = up[at, :].reshape(rows_each - 1, nb, BLK) * main[None]
            scaled[at, :] = block.reshape(span - nb, BLK)
            at = pl.ds(nb * BLK - nb, nb)
            scaled[at, :] = up[at, :] * factors[pl.ds(nb, nb), :]
            at = pl.ds(nb * BLK, 8)
            scaled[at, :] = up[at, :] * factors[pl.ds(2 * nb, 8), :]
            rows += 8
        at = pl.ds(start, rows)
        copy = pltpu.make_async_copy(scaled.at[at], np_out.at[at], sems.at[2 + piece])
        copy.start()
        copies.append(copy)
    for copy in copies:
        copy.wait()


def on_device(
    nz, hidden, grad_query, attn_out, grad_output, flat_params, moment_one, moment_two, step_count
):
    nb = NY * nz
    cells = nb * BLK * BLK
    rows = nb * BLK
    shard_len = flat_params.shape[0]
    step_num = step_count[0].astype(F32)
    fixes = jnp.stack(
        [
            1.0 - jnp.power(jnp.float32(beta_one), step_num),
            1.0 - jnp.power(jnp.float32(beta_two), step_num),
        ]
    )
    vm = lambda shape, dtype=F32: pltpu.VMEM(shape, dtype)
    dma = lambda *shape: pltpu.SemaphoreType.DMA(shape) if shape else pltpu.SemaphoreType.DMA
    grp = nz * CORES
    whole = pl.BlockSpec(memory_space=pltpu.VMEM)
    anywhere = pl.BlockSpec(memory_space=pl.ANY)
    scratch = [
        vm((cells,)), vm((cells,)), vm((cells,)),
        vm((rows + 8, BLK)), vm((rows + 8, BLK)), vm((rows + 8, BLK)),
        vm((nb, BLK, BLK)), vm((nb, BLK, BLK)), vm((nb, BLK, BLK)), vm((nb, BLK, BLK)),
        vm((3, 2, nb, BLK)), vm((2, nb, BLK)),
        vm((NX, BLK, TOK), BF16), vm((NX, 16, TOK), BF16),
        vm((BLK + 32, TOK)), vm((2 * BLK, NX * TOK), BF16), vm((TOK, 2 * BLK), BF16),
        vm((nz, 2, 2 * BLK, NY // 2 * BLK), BF16), vm((NX, nz, NY, TOK, BLK), BF16),
        vm((nz, NY // 2, TOK, BLK)), vm((nz, NY // 2, TOK, BLK)), vm((nz, NY // 2, TOK, BLK)),
        vm((nz, NY // 2, TOK, BLK)), vm((NY, TOK, BLK)),
        vm((8, BLK)), vm((grp * 8, BLK)), vm((2, nb, BLK)),
        vm((8, BLK)), vm((nb, BLK)),
        vm((1, BLK)), vm((NY * grp - 1, 1, BLK)),
        dma(3), dma(3), dma(2), dma(NY, CORES), dma(NY, CORES), dma(3), dma(3),
        dma(NX - 1, 2), dma(NX, 2),
        dma(), dma(), dma(nz), dma(nz), dma(nz, 2), dma(nz, 2),
        dma(nz, 2), dma(nz, 2), dma(NX, nz), dma(NX, nz),
        dma(nz), dma(nz), dma(nz), dma(nz), dma(NY // 2, CORES), dma(NY),
        dma(), dma(),
    ]
    cotangent = jax.ShapeDtypeStruct((64, TOK), BF16)
    flat = jax.ShapeDtypeStruct((rows + 8, BLK), F32)
    tail = pl.BlockSpec((1024,), lambda i: (cells // 1024,))
    outs = pl.pallas_call(
        functools.partial(kernel, nz),
        grid=(1,),
        out_shape=[
            cotangent, cotangent,
            flat, flat, flat,
            jax.ShapeDtypeStruct((2 * nb + 8, BLK), F32),
        ],
        in_specs=[anywhere] + [tail] * 3 + [pl.BlockSpec(memory_space=pltpu.SMEM)] + [anywhere] * 3,
        out_specs=[whole] * 2 + [anywhere] * 3 + [whole],
        scratch_shapes=scratch,
        compiler_params=pltpu.CompilerParams(
            collective_id=0, has_side_effects=True, vmem_limit_bytes=46 * 1024 * 1024
        ),
        cost_estimate=pl.CostEstimate(
            flops=4 * 512 * 128 * 4096, bytes_accessed=6 * 2 * 1024 * 1024, transcendentals=524352
        ),
        name="step",
    )(
        jnp.stack([hidden.T, grad_query.T, attn_out.T, grad_output.T]),
        flat_params, moment_one, moment_two, fixes, flat_params, moment_one, moment_two,
    )
    results = pl.pallas_call(
        functools.partial(finish, nb),
        out_shape=[cotangent] * 2 + [flat] * 3,
        in_specs=[anywhere, anywhere, whole, anywhere, anywhere, whole],
        out_specs=[anywhere] * 5,
        scratch_shapes=[vm((rows + 8, BLK)), dma(8)],
        compiler_params=pltpu.CompilerParams(vmem_limit_bytes=16 * 1024 * 1024),
        name="finish",
    )(*outs)
    grad_hidden, grad_attn = results[0].T, results[1].T
    new_params, new_one, new_two = (part.reshape(-1)[:shard_len] for part in results[2:])
    return (grad_hidden, grad_attn, new_params, new_one, new_two)


def solution(mesh):
    nz = mesh.shape["fsdp"] // (NY * CORES)
    in_specs = (
        P("dp", "fsdp"),
        P("dp", "fsdp"),
        P("dp", "fsdp"),
        P("dp", "fsdp"),
        P("fsdp"),
        P("fsdp"),
        P("fsdp"),
        P(),
    )
    out_specs = (P("dp", "fsdp"), P("dp", "fsdp"), P("fsdp"), P("fsdp"), P("fsdp"))
    return jax.shard_map(
        functools.partial(on_device, nz), mesh=mesh, in_specs=in_specs, out_specs=out_specs, check_vma=False
    )
```

```python
import functools
import math

import jax
import jax.numpy as jnp
from jax import lax
from jax.experimental import pallas as pl
from jax.experimental.pallas import tpu as pltpu
from jax.sharding import PartitionSpec as P

HD = 128
NX = 4
NY = 4
CORES = 2
TOK = 128
BLK = 128

beta_one = 0.9
beta_two = 0.95
adam_eps = 1e-08
learn_rate = 0.02
decay_rate = 0.1
lasso_weight = 2.0
norm_eps = 1e-06

MESH = pl.DeviceIdType.MESH
F32 = jnp.float32
BF16 = jnp.bfloat16
NT = (((1,), (1,)), ((), ()))


def kernel(
    nz, acts, p_tail, m1_tail, m2_tail, fixes, p_hbm, m1_hbm, m2_hbm,
    gh_out, ga_out, up_out, n1_out, n2_out, factor_out,
    p1, m1, m2, p2, o1, o2, pw, m1w, m2w, gw, edge_in, gedge,
    lb, rg, lt, ll, lown,
    wins, rbuf, pb, xs, xr, ring, yb, bias_own, bias_got, bias_add,
    ext_ref, acc_ref, s_own, s_grp,
    in_sem, out_sem, self_sem, s_ry, r_ry, s_lf, r_lf, s_lx, r_lx,
    s_by, r_by, s_rz, r_rz, s_r1, r_r1, s_r2, r_r2, s_rp, r_rp,
    s_sp, r_sp, s_sr, r_sr, s_sy, r_sy, s_sg, r_sg,
):
    h_in, gq_in, a_in, go_in = (acts.at[i] for i in range(4))
    nf = NY * nz * CORES
    nb = NY * nz
    dim = nb * BLK
    half_y = NY // 2
    longs, shorts = nz // 2, nz - 1 - nz // 2
    x = lax.axis_index("dp")
    f = lax.axis_index("fsdp")
    c = f % CORES
    z = (f // CORES) % nz
    y = f // (CORES * nz)
    h = y // half_y
    m = f // 2
    par = f % 2
    k = f // CORES
    sig = 1 - 2 * c

    def fid(yy, zz, cc):
        return (yy * nz + zz) * CORES + cc

    def zw(v):
        return (v + 2 * nz) % nz

    partner = fid(y, z, 1 - c)
    z_long = fid(y, zw(z + sig), c)
    z_short = fid(y, zw(z - sig), c)
    x_up = (x + 1) % NX
    x_down = (x + NX - 1) % NX
    x_far = (x + 2) % NX

    pending = []

    def send(src, dst, ss, rs, xx, ff):
        copy = pltpu.make_async_remote_copy(
            src_ref=src, dst_ref=dst, send_sem=ss, recv_sem=rs,
            device_id=(xx, ff), device_id_type=MESH,
        )
        copy.start()
        return copy

    def send_later(*args):
        pending.append(send(*args))

    def arrive(dst, rs):
        pltpu.make_async_remote_copy(
            src_ref=dst, dst_ref=dst, send_sem=s_by, recv_sem=rs,
            device_id=(x, partner), device_id_type=MESH,
        ).wait_recv()

    cells = nb * BLK * BLK
    loads = [
        pltpu.make_async_copy(src.at[pl.ds(0, cells)], dst, in_sem.at[i])
        for i, (src, dst) in enumerate(((p_hbm, p1), (m1_hbm, m1), (m2_hbm, m2)))
    ]

    barrier = pltpu.get_barrier_semaphore()

    def greet(xx, ff):
        pl.semaphore_signal(barrier, inc=1, device_id=(xx, ff), device_id_type=MESH)

    near_z = sorted({1, nz - 1})
    for dz in near_z:
        greet(x, fid(y, zw(z + dz), c))
    greet(x, partner)
    for dy in range(1, NY):
        for dc in range(CORES):
            greet(x, fid((y + dy) % NY, z, (c + dc) % CORES))
    for dx in range(1, NX):
        greet((x + dx) % NX, f)
    fl = f % (nf // 2)
    row_src = 2 * (fl + 1 - 2 * h) + h
    row_chip = fl + 1 - 2 * h
    has_row = (row_chip >= 0) & (row_chip < nf // 2)
    left_dsts = (k, nf // 2 + k)
    left_srcs = (2 * fl, 2 * fl + 1)
    row_dst_low = k - 1 + 2 * c
    gives_row = (row_dst_low >= 0) & (row_dst_low < nf // 2)
    row_dst = c * (nf // 2) + row_dst_low

    for src in left_srcs:

        @pl.when(src != f)
        def _(src=src):
            greet(x, src)

    @pl.when(has_row)
    def _():
        greet(x, row_src)

    greeted = len(near_z) + 1 + (NY - 1) * CORES + NX - 1
    for dst in left_dsts:
        greeted = greeted + (dst != f).astype(jnp.int32)
    greeted = greeted + gives_row.astype(jnp.int32)
    lane = lax.broadcasted_iota(jnp.int32, (BLK, BLK), 1)
    row = lax.broadcasted_iota(jnp.int32, (BLK, BLK), 0)
    low = lane < 64

    pl.semaphore_wait(barrier, greeted)

    own_half = pl.ds(pl.multiple_of(c * 64, 64), 64)

    def right_sends():
        for yd in range(NY):
            src = h_in if yd < half_y else a_in
            for cc in range(CORES):
                yield yd, cc, src

    for yd, cc, src in right_sends():
        remote = (yd != y) | (cc != c)

        @pl.when(remote)
        def _(yd=yd, cc=cc, src=src):
            send(
                src, rbuf.at[x, z, y, own_half], s_ry.at[yd, cc], r_ry.at[y, c], x, fid(yd, z, cc)
            )

        @pl.when(jnp.logical_not(remote))
        def _(src=src):
            pltpu.make_async_copy(src, rbuf.at[x, z, y, own_half], self_sem.at[0]).start()

    row_part = lambda src: src.at[pl.ds(pl.multiple_of(c * (64 - 16), 16), 16)]
    for i, (src, dst) in enumerate(zip((gq_in, go_in), left_dsts)):

        @pl.when(dst != f)
        def _(i=i, src=src, dst=dst):
            send(src, lb.at[x, own_half], s_lf.at[i], r_lf.at[c], x, dst)

        @pl.when(dst == f)
        def _(src=src):
            pltpu.make_async_copy(src, lb.at[x, own_half], self_sem.at[1]).start()

        @pl.when(gives_row & (c == i))
        def _(src=src):
            send(row_part(src), rg.at[x], s_lf.at[2], r_lf.at[2], x, row_dst)

    @pl.when(jnp.logical_not(has_row))
    def _():
        rg[x] = jnp.zeros((16, TOK), BF16)

    loads[0].start()

    loads[0].wait()
    group_cells = 8 * dim

    @pl.loop(0, BLK // 8)
    def _(i):
        some = p1[pl.ds(i * group_cells, group_cells)].reshape(8, nb, BLK)
        pw[:, pl.ds(pl.multiple_of(i * 8, 8), 8), :] = jnp.swapaxes(some, 0, 1)

    pair = lambda cc: pl.ds(half_y * cc, half_y)
    def own_quad():
        for yy in range(NY):
            for cc in range(CORES):
                remote = (yy != y) | (cc != c)
                half = rbuf.at[x, z, yy, pl.ds(cc * 64, 64)]

                @pl.when(remote)
                def _(yy=yy, cc=cc, half=half):
                    arrive(half, r_ry.at[yy, cc])

        pltpu.make_async_copy(h_in, rbuf.at[x, z, y, own_half], self_sem.at[0]).wait()

    def z_quad(r):
        out = []
        if r == 0:
            return [(0, z)]
        if r <= longs:
            out.append((2 * r - 1, zw(z - sig * r)))
        if r <= shorts:
            out.append((2 * r, zw(z + sig * r)))
        return out

    def round_a(r):
        for idx, zq in z_quad(r):
            ref = rbuf.at[x, zq, pair(c)]
            if r > 0:
                arrive(ref, r_rz.at[idx])
            is_long = r == 0 or idx % 2 == 1
            is_short = r == 0 or idx % 2 == 0
            if is_long and r < longs:
                send_later(ref, ref, s_rz.at[2 * r + 1], r_rz.at[2 * r + 1], x, z_long)
            if is_short and r < shorts:
                send_later(ref, ref, s_rz.at[2 * r + 2], r_rz.at[2 * r + 2], x, z_short)
            send_later(ref, ref, s_r1.at[idx, 0], r_r1.at[idx, 0], x_up, f)
            send_later(ref, ref, s_r1.at[idx, 1], r_r1.at[idx, 1], x_down, f)
            if r > 0:
                send_later(ref, ref, s_rp.at[x, zq], r_rp.at[x, zq], x, partner)

    def round_x1(r):
        for idx, zq in z_quad(r):
            ways = ((x_down, x_up), (x_up, x_down))
            for way, (frm, to) in enumerate(ways):
                arrive(rbuf.at[frm, zq, pair(c)], r_r1.at[idx, way])
                part = rbuf.at[frm, zq, half_y * c + way]
                send_later(part, part, s_r2.at[idx, way], r_r2.at[idx, way], to, f)
            for frm, _ in ways:
                ref = rbuf.at[frm, zq, pair(c)]
                send_later(ref, ref, s_rp.at[frm, zq], r_rp.at[frm, zq], x, partner)

    def round_x2(r):
        for idx, zq in z_quad(r):
            ref = rbuf.at[x_far, zq, pair(c)]
            for way in range(2):
                arrive(rbuf.at[x_far, zq, half_y * c + way], r_r2.at[idx, way])
            send_later(ref, ref, s_rp.at[x_far, zq], r_rp.at[x_far, zq], x, partner)

    own_quad()
    round_a(0)

    lane_row = lax.broadcasted_iota(jnp.int32, (1, BLK), 1)

    def tail_row(ref):
        return jnp.where(lane_row < 64, ref[...].reshape(8, BLK)[0:1], 0.0)

    tail_p = tail_row(p_tail)
    tail_here = jnp.where(
        par == 1, pltpu.roll(jnp.broadcast_to(tail_p, (8, BLK)), 64, 1)[0:1], tail_p
    )

    def window_block(j):
        first = pw[(j - m + nb) % nb]
        second = pw[(j - m - 1 + nb) % nb]
        mixed = pltpu.roll(jnp.where(low, first, second), 64, 1)
        block = jnp.where(par == 1, mixed, first)
        column = j * BLK + lane
        carried = column < 64 * f
        top = jnp.where(carried, 0.0, block)
        bottom = jnp.where(carried, block, 0.0)
        is_tail = (row == BLK - 1) & (column >= 64 * f) & (column < 64 * f + 64)
        bottom = jnp.where(is_tail, tail_here, bottom)
        return jnp.concatenate([top, bottom], axis=0).astype(BF16)

    @pl.loop(0, nz)
    def _(d):
        for hh in range(2):
            for i in range(half_y):
                wins[d, hh, :, i * BLK : (i + 1) * BLK] = window_block((half_y * hh + i) * nz + d)

    for cc, src in enumerate(left_srcs):

        @pl.when(src != f)
        def _(cc=cc):
            arrive(lb.at[x, pl.ds(cc * 64, 64)], r_lf.at[cc])

        @pl.when(src == f)
        def _():
            pltpu.make_async_copy(gq_in, lb.at[x, own_half], self_sem.at[1]).wait()

    @pl.when(has_row)
    def _():
        arrive(rg.at[x], r_lf.at[2])

    for dx in range(1, NX):
        xx = (x + dx) % NX
        send_later(lb.at[x], lb.at[x], s_lx.at[dx - 1, 0], r_lx.at[x, 0], xx, f)
        send_later(rg.at[x], rg.at[x], s_lx.at[dx - 1, 1], r_lx.at[x, 1], xx, f)

    def build_left(xx):
        lt[pl.ds(0, 16), :] = rg[xx].astype(F32)
        lt[pl.ds(16, BLK), :] = lb[xx].astype(F32)
        lt[pl.ds(16 + BLK, 16), :] = rg[xx].astype(F32)
        before = lt[pl.ds(15, BLK), :]
        middle = lt[pl.ds(16, BLK), :]
        after = lt[pl.ds(17, BLK), :]
        zero = jnp.where(h == 0, middle, before)
        one = jnp.where(h == 0, after, middle)
        return zero, one

    zero, one = build_left(x)
    lown[:, pl.ds(0, BLK)] = jnp.transpose(zero).astype(BF16)
    lown[:, pl.ds(BLK, BLK)] = jnp.transpose(one).astype(BF16)

    def partial_chunk(d):
        for mine in range(2):
            hh = c if mine == 0 else 1 - c
            part = jnp.dot(lown[...], wins[d, hh], preferred_element_type=F32)
            for i in range(half_y):
                target = pb if mine == 0 else xs
                target[d, i] = part[:, i * BLK : (i + 1) * BLK]
        send_later(xs.at[d], xr.at[d], s_sp.at[d], r_sp.at[d], x, partner)

    def round_c(r):
        if r >= longs:
            return
        partial_chunk(zw(z + sig * (longs - r)))
        partial_chunk(zw(z - sig * (shorts - r)))

    def chip_sum(d):
        arrive(xr.at[d], r_sp.at[d])
        return pb[d] + xr[d]

    def round_e(r):
        for way, (hops, to, sign) in enumerate(((longs, z_long, 1), (shorts, z_short, -1))):
            if r >= hops:
                continue
            d = zw(z + sig * sign * (hops - r))
            slot = 2 * r + way
            if r == 0:
                pb[d] = chip_sum(d)
                src = pb.at[d]
            else:
                before = slot - 2
                arrive(ring.at[before], r_sr.at[before])
                ring[before] = ring[before] + chip_sum(d)
                src = ring.at[before]
            send_later(src, ring.at[slot], s_sr.at[slot], r_sr.at[slot], x, to)

    def finish_sums():
        total = chip_sum(z)
        slot = 2 * (longs - 1)
        arrive(ring.at[slot], r_sr.at[slot])
        total = total + ring[slot]
        if shorts:
            slot = 2 * (shorts - 1) + 1
            arrive(ring.at[slot], r_sr.at[slot])
            total = total + ring[slot]
        pb[z] = total
        for i in range(half_y):
            for cc in range(CORES):
                yd = half_y * c + i

                @pl.when((yd != y) | (cc != c))
                def _(i=i, cc=cc, yd=yd):
                    send(pb.at[z, i], yb.at[y], s_sy.at[i, cc], r_sy.at[y], x, fid(yd, z, cc))

        @pl.when(h == c)
        def _():
            yb[y] = pb[z, y % half_y]

    def write_cotangents():
        for yy in range(NY):

            @pl.when((yy != y) | (h != c))
            def _(yy=yy):
                arrive(yb.at[yy], r_sy.at[yy])

        for out, base_y in ((gh_out, 0), (ga_out, half_y)):
            total = yb[base_y]
            for i in range(1, half_y):
                total = total + yb[base_y + i]
            total = jnp.transpose(total)
            out[...] = jnp.where(c == 1, total[64:], total[:64]).astype(BF16)

    def full_left():
        for xx in range(NX):

            @pl.when(xx != x)
            def _(xx=xx):
                arrive(lb.at[xx], r_lx.at[xx, 0])
                arrive(rg.at[xx], r_lx.at[xx, 1])

            zero, one = build_left(xx)
            ll[pl.ds(0, BLK), pl.ds(xx * TOK, TOK)] = zero.astype(BF16)
            ll[pl.ds(BLK, BLK), pl.ds(xx * TOK, TOK)] = one.astype(BF16)
        bias_own[...] = lax.dot_general(
            jnp.ones((8, NX * TOK), BF16), ll[pl.ds(0, BLK), :], NT, preferred_element_type=F32
        )

    quarter = nf // 4
    bias_dst = nf // 2 - 1 + f // quarter
    bias_slot = pl.ds(pl.multiple_of((f % quarter) * 8, 8), 8)

    def bias_on():
        @pl.when(f < nf // 2)
        def _():
            send(bias_own, bias_got.at[bias_slot], s_by, r_by, x, bias_dst)

    ext_ref[...] = jnp.zeros((8, BLK), F32)

    def gradient_quad(r):
        for _, zq in z_quad(r):
            for xx in range(NX):
                if r == 0:

                    @pl.when(xx != x)
                    def _(xx=xx, zq=zq):
                        arrive(rbuf.at[xx, zq, pair(1 - c)], r_rp.at[xx, zq])
                else:
                    arrive(rbuf.at[xx, zq, pair(1 - c)], r_rp.at[xx, zq])
            for yy in range(0, NY, 2):
                wide = jnp.concatenate(
                    [
                        jnp.concatenate([rbuf[xx, zq, yy], rbuf[xx, zq, yy + 1]], axis=0)
                        for xx in range(NX)
                    ],
                    axis=1,
                )
                both = lax.dot_general(ll[...], wide, NT, preferred_element_type=F32)
                for i in range(2):
                    j = (yy + i) * nz + zq
                    p_zero = both[:BLK, i * BLK : (i + 1) * BLK]
                    p_one = both[BLK:, i * BLK : (i + 1) * BLK]
                    carried = j * BLK + lane < 64 * f
                    gw[j] = jnp.where(carried, p_one, p_zero)
                    ext_ref[...] = ext_ref[...] + jnp.where(
                        j == m, p_one[BLK - 8 :, :], jnp.zeros((8, BLK), F32)
                    )

    one_scale = 1.0 / fixes[0]
    two_scale = 1.0 / fixes[1]

    def adam(grad, param, mom_one, mom_two):
        new_one = beta_one * mom_one + (1.0 - beta_one) * grad
        new_two = beta_two * mom_two + (1.0 - beta_two) * grad * grad
        direction = (new_one * one_scale) / (jnp.sqrt(new_two * two_scale) + adam_eps)
        return new_one, new_two, param - learn_rate * (direction + decay_rate * param)

    rows_each = 8
    span = rows_each * nb

    def by_block(source, target):
        @pl.loop(0, BLK // rows_each)
        def _(i):
            flat = pl.ds(pl.multiple_of(i * span * BLK, span * BLK), span * BLK)
            some = source[flat].reshape(rows_each, nb, BLK)
            at = pl.ds(pl.multiple_of(i * rows_each, rows_each), rows_each)
            target[:, at, :] = jnp.swapaxes(some, 0, 1)

    def moments():
        loads[1].wait()
        loads[2].wait()
        by_block(m1, m1w)
        by_block(m2, m2w)
        for n, ref in enumerate((pw, m1w, m2w)):
            edge_in[n, 0] = jnp.swapaxes(ref[:, pl.ds(0, 8), :], 0, 1)[0]
            edge_in[n, 1] = jnp.swapaxes(ref[:, pl.ds(BLK - 8, 8), :], 0, 1)[7]

    inner = (row > 0) & (row < BLK - 1)

    def adam_blocks(zc):
        for yy in range(NY):
            j = yy * nz + zc
            first = gw[j]
            second = gw[(j + 1) % nb]
            mixed = pltpu.roll(jnp.where(low, second, first), 64, 1)
            grad = jnp.where(par == 1, mixed, first)
            b = (j - m + nb) % nb
            new_one, new_two, updated = adam(grad, pw[b], m1w[b], m2w[b])
            m1w[b] = new_one
            m2w[b] = new_two
            pw[b] = updated
            squares = jnp.where(inner, updated * updated, 0.0)
            acc_ref[pl.ds(b, 1), :] = jnp.sum(squares, axis=0, keepdims=True)
            gedge[0, pl.ds(b, 1), :] = grad[:1]
            gedge[1, pl.ds(b, 1), :] = grad[BLK - 1 :]

    def gradient(r):
        gradient_quad(r)
        if 0 < r <= longs:
            adam_blocks(zw(z - r))
            adam_blocks(zw(z + r - 1))

    bias_add[...] = jnp.zeros((2, nb, BLK), F32)

    def bias_rows():
        half = nb // 2

        @pl.when((f == nf // 2) | (f == nf // 2 - 1))
        def _():
            arrive(bias_got, r_by)
            sums = bias_got[pl.ds(0, half, stride=8), :]

            @pl.when(f == nf // 2)
            def _():
                bias_add[0, pl.ds(0, half)] = sums

            @pl.when(f == nf // 2 - 1)
            def _():
                turned = pltpu.roll(sums, 64, 1)
                index = lax.broadcasted_iota(jnp.int32, (half, BLK), 0)
                before = jnp.where(index == 0, 0.0, pltpu.roll(turned, 1, 0))
                left_half = lax.broadcasted_iota(jnp.int32, (half, BLK), 1) < 64
                bias_add[1, pl.ds(half, half)] = jnp.where(left_half, before, turned)
                ext_ref[...] = ext_ref[...] + sums[half - 1 : half]

    round_c(0)
    round_c(1)
    round_a(1)
    round_e(0)
    round_x1(0)
    round_c(2)
    round_a(2)
    round_x1(1)
    round_x2(0)
    round_c(3)
    full_left()
    loads[1].start()
    loads[2].start()
    round_a(3)
    round_e(1)
    round_x1(2)
    round_x2(1)
    moments()
    gradient(0)
    round_a(4)
    bias_on()
    round_e(2)
    round_x1(3)
    round_x2(2)
    gradient(1)
    round_x1(4)
    round_x2(3)
    round_e(3)
    gradient(2)
    round_x2(4)
    gradient(3)
    gradient(4)
    bias_rows()

    def edge_step(e):
        return adam(gedge[e] + bias_add[e], edge_in[0, e], edge_in[1, e], edge_in[2, e])

    edges = [edge_step(e) for e in range(2)]
    acc_main = acc_ref[...] + edges[0][2] * edges[0][2]
    acc_last = edges[1][2] * edges[1][2]
    ext_row = ext_ref[...]
    ext_row = jnp.where(par == 1, pltpu.roll(ext_row, 64, 1), ext_row)[7:8]
    ext_one, ext_two, ext_up = adam(
        ext_row, tail_p, tail_row(m1_tail), tail_row(m2_tail)
    )
    o1[pl.ds(nb * BLK, 8), :] = jnp.broadcast_to(ext_one, (8, BLK))
    o2[pl.ds(nb * BLK, 8), :] = jnp.broadcast_to(ext_two, (8, BLK))
    p2[pl.ds(nb * BLK, 8), :] = jnp.broadcast_to(ext_up, (8, BLK))
    writes = [
        pltpu.make_async_copy(ref, out, out_sem.at[sem])
        for ref, out, sem in ((o1, n1_out, 0), (o2, n2_out, 1), (p2, up_out, 2))
    ]

    heads = lax.broadcasted_iota(jnp.int32, (nb, BLK), 1)
    blocks = lax.broadcasted_iota(jnp.int32, (nb, BLK), 0)
    low_b = heads < 64
    ext_sq = jnp.sum(jnp.where(lane_row < 64, ext_up * ext_up, 0.0), axis=1, keepdims=True)

    def head_of(part):
        spot = f + 2 * blocks + part
        carry = spot // nf
        by_column = (spot % nf) // 2
        main = jnp.where(h == 0, f, by_column)
        last_q = jnp.where(f + carry < nf // 2, f + carry, by_column)
        return main, last_q

    ext_head = jnp.where(f + 1 < nf // 2, f + 1, f // 2)
    total = jnp.where(lane_row == ext_head, ext_sq, 0.0)
    maps = [head_of(0), head_of(1)]
    for part in range(2):
        inside = low_b if part == 0 else jnp.logical_not(low_b)
        for which, acc in enumerate((acc_main, acc_last)):
            sums = jnp.sum(jnp.where(inside, acc, 0.0), axis=1, keepdims=True)
            total = total + jnp.sum(
                jnp.where(maps[part][which] == heads, sums, 0.0), axis=0, keepdims=True
            )
    s_own[...] = total
    offsets = [
        (dy, dz, dc)
        for dy in range(NY)
        for dz in range(nz)
        for dc in range(CORES)
        if (dy, dz, dc) != (0, 0, 0)
    ]
    offsets.sort(key=lambda o: -(min(o[0], NY - o[0]) + min(o[1], nz - o[1])))
    for i, (dy, dz, dc) in enumerate(offsets):
        target = fid((y + dy) % NY, zw(z + dz), (c + dc) % CORES)
        send(s_own, s_grp.at[i], s_sg, r_sg, x, target)
    finish_sums()
    for n, (blocked, flat) in enumerate(((m1w, o1), (m2w, o2), (pw, p2))):

        @pl.loop(0, BLK // rows_each)
        def _(i):
            some = blocked[:, pl.ds(pl.multiple_of(i * rows_each, rows_each), rows_each), :]
            at = pl.ds(pl.multiple_of(i * span, span), span)
            flat[at, :] = jnp.swapaxes(some, 0, 1).reshape(span, BLK)

        flat[pl.ds(0, nb), :] = edges[0][n]
        flat[pl.ds((BLK - 1) * nb, nb), :] = edges[1][n]
        writes[n].start()

    arrive(s_grp, r_sg)
    sumsq = s_own[...] + jnp.sum(s_grp[...], axis=0)
    threshold = learn_rate * lasso_weight * math.sqrt(2 * HD * dim + HD)
    shrink = jnp.maximum(1.0 - threshold / jnp.sqrt(sumsq + norm_eps), 0.0)

    def factor(which):
        sides = [
            jnp.sum(jnp.where(maps[part][which] == heads, shrink, 0.0), axis=1, keepdims=True)
            for part in range(2)
        ]
        return jnp.where(low_b, sides[0], sides[1])

    factor_out[pl.ds(0, nb), :] = factor(0)
    factor_out[pl.ds(nb, nb), :] = factor(1)
    ext_shrink = jnp.sum(jnp.where(lane_row == ext_head, shrink, 0.0), axis=1, keepdims=True)
    factor_out[pl.ds(2 * nb, 8), :] = jnp.broadcast_to(ext_shrink, (8, BLK))

    write_cotangents()

    def sent(src, ss):
        pltpu.make_async_remote_copy(
            src_ref=src, dst_ref=src, send_sem=ss, recv_sem=r_by,
            device_id=(x, partner), device_id_type=MESH,
        ).wait_send()

    sent(s_grp, s_sg)
    for copy in pending:
        copy.wait_send()
    for yd, cc, src in right_sends():

        @pl.when((yd != y) | (cc != c))
        def _(yd=yd, cc=cc, src=src):
            sent(src, s_ry.at[yd, cc])

    for i in range(half_y):
        for cc in range(CORES):
            yd = half_y * c + i

            @pl.when((yd != y) | (cc != c))
            def _(i=i, cc=cc):
                sent(pb.at[z, i], s_sy.at[i, cc])

    for i, (src, dst) in enumerate(zip((gq_in, go_in), left_dsts)):

        @pl.when(dst != f)
        def _(i=i, src=src):
            sent(src, s_lf.at[i])

    @pl.when(gives_row)
    def _():
        sent(row_part(gq_in), s_lf.at[2])

    @pl.when(f < nf // 2)
    def _():
        sent(bias_own, s_by)

    for write in writes:
        write.wait()


def finish(nb, gh, ga, up, n1, n2, factors, gh_out, ga_out, np_out, n1_out, n2_out, scaled, sems):
    copies = [
        pltpu.make_async_copy(gh, gh_out, sems.at[6]),
        pltpu.make_async_copy(ga, ga_out, sems.at[7]),
        pltpu.make_async_copy(n1, n1_out, sems.at[0]),
        pltpu.make_async_copy(n2, n2_out, sems.at[1]),
    ]
    for copy in copies:
        copy.start()
    pieces, rows_each = 4, 4
    span = rows_each * nb
    steps = BLK // rows_each // pieces
    main = factors[pl.ds(0, nb), :]
    for piece in range(pieces):
        start = piece * steps * span
        full = steps - 1 if piece == pieces - 1 else steps

        @pl.loop(0, full)
        def _(i):
            at = pl.ds(pl.multiple_of(start + i * span, span), span)
            block = up[at, :].reshape(rows_each, nb, BLK) * factors[pl.ds(0, nb), :][None]
            scaled[at, :] = block.reshape(span, BLK)

        rows = steps * span
        if piece == pieces - 1:
            at = pl.ds(start + full * span, span - nb)
            block = up[at, :].reshape(rows_each - 1, nb, BLK) * main[None]
            scaled[at, :] = block.reshape(span - nb, BLK)
            at = pl.ds(nb * BLK - nb, nb)
            scaled[at, :] = up[at, :] * factors[pl.ds(nb, nb), :]
            at = pl.ds(nb * BLK, 8)
            scaled[at, :] = up[at, :] * factors[pl.ds(2 * nb, 8), :]
            rows += 8
        at = pl.ds(start, rows)
        copy = pltpu.make_async_copy(scaled.at[at], np_out.at[at], sems.at[2 + piece])
        copy.start()
        copies.append(copy)
    for copy in copies:
        copy.wait()


def on_device(
    nz, hidden, grad_query, attn_out, grad_output, flat_params, moment_one, moment_two, step_count
):
    nb = NY * nz
    cells = nb * BLK * BLK
    rows = nb * BLK
    shard_len = flat_params.shape[0]
    step_num = step_count[0].astype(F32)
    fixes = jnp.stack(
        [
            1.0 - jnp.power(jnp.float32(beta_one), step_num),
            1.0 - jnp.power(jnp.float32(beta_two), step_num),
        ]
    )
    vm = lambda shape, dtype=F32: pltpu.VMEM(shape, dtype)
    dma = lambda *shape: pltpu.SemaphoreType.DMA(shape) if shape else pltpu.SemaphoreType.DMA
    grp = nz * CORES
    whole = pl.BlockSpec(memory_space=pltpu.VMEM)
    anywhere = pl.BlockSpec(memory_space=pl.ANY)
    scratch = [
        vm((cells,)), vm((cells,)), vm((cells,)),
        vm((rows + 8, BLK)), vm((rows + 8, BLK)), vm((rows + 8, BLK)),
        vm((nb, BLK, BLK)), vm((nb, BLK, BLK)), vm((nb, BLK, BLK)), vm((nb, BLK, BLK)),
        vm((3, 2, nb, BLK)), vm((2, nb, BLK)),
        vm((NX, BLK, TOK), BF16), vm((NX, 16, TOK), BF16),
        vm((BLK + 32, TOK)), vm((2 * BLK, NX * TOK), BF16), vm((TOK, 2 * BLK), BF16),
        vm((nz, 2, 2 * BLK, NY // 2 * BLK), BF16), vm((NX, nz, NY, TOK, BLK), BF16),
        vm((nz, NY // 2, TOK, BLK)), vm((nz, NY // 2, TOK, BLK)), vm((nz, NY // 2, TOK, BLK)),
        vm((nz, NY // 2, TOK, BLK)), vm((NY, TOK, BLK)),
        vm((8, BLK)), vm((grp * 8, BLK)), vm((2, nb, BLK)),
        vm((8, BLK)), vm((nb, BLK)),
        vm((1, BLK)), vm((NY * grp - 1, 1, BLK)),
        dma(3), dma(3), dma(2), dma(NY, CORES), dma(NY, CORES), dma(3), dma(3),
        dma(NX - 1, 2), dma(NX, 2),
        dma(), dma(), dma(nz), dma(nz), dma(nz, 2), dma(nz, 2),
        dma(nz, 2), dma(nz, 2), dma(NX, nz), dma(NX, nz),
        dma(nz), dma(nz), dma(nz), dma(nz), dma(NY // 2, CORES), dma(NY),
        dma(), dma(),
    ]
    cotangent = jax.ShapeDtypeStruct((64, TOK), BF16)
    flat = jax.ShapeDtypeStruct((rows + 8, BLK), F32)
    tail = pl.BlockSpec((1024,), lambda i: (cells // 1024,))
    outs = pl.pallas_call(
        functools.partial(kernel, nz),
        grid=(1,),
        out_shape=[
            cotangent, cotangent,
            flat, flat, flat,
            jax.ShapeDtypeStruct((2 * nb + 8, BLK), F32),
        ],
        in_specs=[anywhere] + [tail] * 3 + [pl.BlockSpec(memory_space=pltpu.SMEM)] + [anywhere] * 3,
        out_specs=[whole] * 2 + [anywhere] * 3 + [whole],
        scratch_shapes=scratch,
        compiler_params=pltpu.CompilerParams(
            collective_id=0, has_side_effects=True, vmem_limit_bytes=46 * 1024 * 1024
        ),
        cost_estimate=pl.CostEstimate(
            flops=4 * 512 * 128 * 4096, bytes_accessed=6 * 2 * 1024 * 1024, transcendentals=524352
        ),
        name="step",
    )(
        jnp.stack([hidden.T, grad_query.T, attn_out.T, grad_output.T]),
        flat_params, moment_one, moment_two, fixes, flat_params, moment_one, moment_two,
    )
    results = pl.pallas_call(
        functools.partial(finish, nb),
        out_shape=[cotangent] * 2 + [flat] * 3,
        in_specs=[anywhere, anywhere, whole, anywhere, anywhere, whole],
        out_specs=[anywhere] * 5,
        scratch_shapes=[vm((rows + 8, BLK)), dma(8)],
        compiler_params=pltpu.CompilerParams(vmem_limit_bytes=16 * 1024 * 1024),
        name="finish",
    )(*outs)
    grad_hidden, grad_attn = results[0].T, results[1].T
    new_params, new_one, new_two = (part.reshape(-1)[:shard_len] for part in results[2:])
    return (grad_hidden, grad_attn, new_params, new_one, new_two)


def solution(mesh):
    nz = mesh.shape["fsdp"] // (NY * CORES)
    in_specs = (
        P("dp", "fsdp"),
        P("dp", "fsdp"),
        P("dp", "fsdp"),
        P("dp", "fsdp"),
        P("fsdp"),
        P("fsdp"),
        P("fsdp"),
        P(),
    )
    out_specs = (P("dp", "fsdp"), P("dp", "fsdp"), P("fsdp"), P("fsdp"), P("fsdp"))
    return jax.shard_map(
        functools.partial(on_device, nz), mesh=mesh, in_specs=in_specs, out_specs=out_specs, check_vma=False
    )
```
